512 devices in a mesh: dp: 32 (over y, x, core), cent: 16 (over z).
Axes of the slice: x: 4, y: 4, z: 16, core: 2. Of those that a mesh axis runs over, the one named last changes fastest.
Arguments:
- embeddings: bfloat16 [61440, 1024], P('dp'), may hold values from -32 to 32
- centroids: float32 [2048, 1024], P('cent'), may hold values from -1.5 to 1.5
Outputs:
- new_centroids: float32 [2048, 1024], P('cent')
- row_energy: float32 [61440], P('dp')
The draws below stay inside these ranges and needn't reach their ends.
All inputs are finite; a program needn't handle non-finite values.
Results may differ from the reference program's by a relative error of at most 0.00075.
Values sent between devices are 32-bit elements; how exact they have to be, the bound alone decides.
A program may use at most 64 MiB of HBM per device.

```python
import math
import jax
import jax.numpy as jnp
from jax import lax

D = 1024
K = 2048
ROW_DEV = 1920
ITERS = 2
ROWS = 61440
N_DP = 32


def shared_centroids(key):
    key_scale, key_base = jax.random.split(key, 2)
    scales = jnp.exp(jax.random.uniform(key_scale, (K, 1), jnp.float32, math.log(0.05), math.log(0.15)))
    base = jax.random.normal(key_base, (K, D), jnp.float32) * scales
    return base


def draw_centroids(key, part):
    base = shared_centroids(key)
    return base


def draw_embeddings(key, part):
    key = jax.random.fold_in(key, 3)
    key_rows, key_noise = jax.random.split(key, 2)
    row_scale = jnp.exp(jax.random.uniform(key_rows, (ROWS, 1), jnp.float32, math.log(0.4), math.log(4.0)))
    rows = jax.random.normal(key_noise, (ROWS, D), jnp.float32) * row_scale
    return rows.astype(jnp.bfloat16)


def setup_inputs(seed: int = 0) -> dict:
    key_of = jax.random.split(jax.random.key(seed), 3)
    embeddings = draw_embeddings(jax.random.fold_in(key_of[2], 71), 0)
    centroids = draw_centroids(jax.random.fold_in(key_of[2], 71), 0)
    return dict(embeddings=embeddings, centroids=centroids)


prior_count = 2.0


def reference(embeddings, centroids):
    current = centroids
    blocks = embeddings.reshape(N_DP, ROW_DEV, D)
    energies = jnp.zeros((N_DP, ROW_DEV), jnp.float32)
    for step in range(ITERS):
        offset = 0.5 * jnp.sum(current * current, axis=1)

        def visit(carry, block):
            numer, mass = carry
            rows = block.astype(jnp.float32)
            logits = lax.dot_general(rows, current, (((1,), (1,)), ((), ())), precision=lax.Precision.HIGHEST, preferred_element_type=jnp.float32) - offset[None, :]
            top = jnp.max(logits, axis=1)
            total = jnp.sum(jnp.exp(logits - top[:, None]), axis=1)
            energy = top + jnp.log(total)
            weights = jnp.exp(logits - energy[:, None])
            numer = numer + lax.dot_general(weights, rows, (((0,), (0,)), ((), ())), precision=lax.Precision.HIGHEST, preferred_element_type=jnp.float32)
            mass = mass + jnp.sum(weights, axis=0)
            return (numer, mass), energy

        start = (jnp.zeros((K, D), jnp.float32), jnp.zeros((K,), jnp.float32))
        (numer, mass), energies = lax.scan(visit, start, blocks)
        current = (numer + prior_count * current) / (mass + prior_count)[:, None]
    return current, energies.reshape(ROWS)
```

```python
import jax
import jax.numpy as jnp
from jax import lax
from jax.experimental import pallas as pl
from jax.experimental.pallas import tpu as pltpu
from jax.sharding import PartitionSpec as P

MESH = pl.DeviceIdType.MESH
ITERS = 2
PRIOR = 2.0
N = 4
ZG = 4
ROWS = 1920
D = 1024
K = 128
PIECE = 128
HALF = D // 2
Q = 2
CW = HALF // Q
CHUNKS = ((0, 8), (8, 15))
NT = (((1,), (1,)), ((), ()))
NN = (((1,), (0,)), ((), ()))


def dot(a, b, dims):
    return lax.dot_general(a, b, dims, preferred_element_type=jnp.float32)


def split(v):
    hi = v.astype(jnp.bfloat16)
    lo = (v - hi.astype(jnp.float32)).astype(jnp.bfloat16)
    return hi, lo


def kernel(
    x_hbm, c_hbm, out_c, out_e,
    xv, cur, cs, pbuf, ws, macc, mst, est, zrecv,
    nacc, nsend, crecv, sbuf, arecv, mbuf, mr0, mr1,
    ld, out_sem, z_send, z_recv,
    c_send, c_recv, a_send, a_recv, g_send, g_recv, gc_send, gc_recv,
    m_send, m_recv,
):
    dp = lax.axis_index("dp")
    z = lax.axis_index("cent")
    core = lax.rem(dp, 2)
    chip = dp // 2
    cx = lax.rem(chip, N)
    cy = chip // N
    zg = z // ZG
    zl = lax.rem(z, ZG)
    other = (dp + 1 - 2 * core, z)

    def chip_at(dx, dy):
        return lax.rem(cy + dy, N) * N + lax.rem(cx + dx, N)

    moves = [(dx, dy) for dx in range(N) for dy in range(N) if dx or dy]
    moves.sort(key=lambda v: -(min(v[0], N - v[0]) + min(v[1], N - v[1])))
    chips = [chip_at(dx, dy) for dx, dy in moves]
    planes = [(2 * c + core, z) for c in chips]
    stages = (
        [(dp, zg * ZG + lax.rem(zl + d, ZG)) for d in range(1, ZG)],
        [(dp, lax.rem(zg + d, ZG) * ZG + zl) for d in range(1, ZG)],
    )

    def push(src, dst, send, recv, device):
        pltpu.make_async_remote_copy(
            src_ref=src, dst_ref=dst, send_sem=send, recv_sem=recv,
            device_id=device, device_id_type=MESH,
        ).start()

    def await_bytes(ref, sem):
        pltpu.make_async_copy(ref, ref, sem).wait()

    barrier = pltpu.get_barrier_semaphore()
    peers = [other] + planes + stages[0] + stages[1]
    for device in peers:
        pl.semaphore_signal(barrier, inc=1, device_id=device, device_id_type=MESH)

    load_c = pltpu.make_async_copy(c_hbm, cur.at[0], ld.at[0])
    load_c.start()
    loads = []
    for n, (lo, hi) in enumerate(CHUNKS):
        rows = pl.ds(lo * PIECE, (hi - lo) * PIECE)
        loads.append(pltpu.make_async_copy(x_hbm.at[rows], xv.at[rows], ld.at[n + 1]))
        loads[-1].start()

    def own_cols(q):
        return pl.ds(pl.multiple_of(core * HALF + q * CW, CW), CW)

    def far_cols(q):
        return pl.ds(pl.multiple_of((1 - core) * HALF + q * CW, CW), CW)

    own_half = pl.ds(pl.multiple_of(core * HALF, HALF), HALF)
    far_half = pl.ds(pl.multiple_of((1 - core) * HALF, HALF), HALF)
    base = pl.multiple_of(chip * 8, 8)
    mine = pl.ds(base, 8)

    def split_centroids(it, cols):
        c = cur[it, :, cols]
        hi, lo = split(c)
        cs[0:K, cols] = hi
        cs[K : 2 * K, cols] = lo
        return 0.5 * jnp.sum(c * c, axis=1, keepdims=True)

    def stats(it, n, l, r):
        i = r - CHUNKS[n][0]
        m = jnp.max(l, axis=0, keepdims=True)
        p = jnp.exp(l - m)
        s = jnp.sum(p, axis=0, keepdims=True)
        pbuf[r] = p
        mst[n, i : i + 1] = m
        est[it, n, 0, i : i + 1] = m + jnp.log(s)

    def product(rows, cols):
        both = dot(cs[:, cols], xv[rows, cols], NT)
        return both[0:K] + both[K : 2 * K]

    def logits(it, n):
        lo, hi = CHUNKS[n]
        for r0 in range(lo, hi, 2):
            size = min(2, hi - r0)
            rows = pl.ds(r0 * PIECE, size * PIECE)
            l = product(rows, pl.ds(0, D) if it == 0 else far_half) - offset
            for j in range(size):
                part = l[:, j * PIECE : (j + 1) * PIECE]
                stats(it, n, part if it == 0 else part + pbuf[r0 + j], r0 + j)

    def z_push(it, n, stage):
        for d, device in enumerate(stages[stage]):
            push(est.at[it, n, stage], zrecv.at[it, n, stage, d], z_send.at[it, n, stage], z_recv.at[it, n, stage], device)

    def z_join(it, n, stage):
        await_bytes(zrecv.at[it, n, stage], z_recv.at[it, n, stage])
        e = [est[it, n, stage]] + [zrecv[it, n, stage, d] for d in range(ZG - 1)]
        m = jnp.maximum(jnp.maximum(e[0], e[1]), jnp.maximum(e[2], e[3]))
        s = (jnp.exp(e[0] - m) + jnp.exp(e[1] - m)) + (jnp.exp(e[2] - m) + jnp.exp(e[3] - m))
        est[it, n, stage + 1] = m + jnp.log(s)

    def weigh(it, n):
        lo, hi = CHUNKS[n]
        f = jnp.exp(mst[n] - est[it, n, 2])
        for r in range(lo, hi):
            w = pbuf[r] * f[r - lo : r - lo + 1]
            hi_w, lo_w = split(w)
            cols = pl.ds(r * PIECE, PIECE)
            ws[0:K, cols] = hi_w
            ws[K : 2 * K, cols] = lo_w
            macc[...] += w

    def numer(n, cols):
        lo, hi = CHUNKS[n]
        rows = pl.ds(lo * PIECE, (hi - lo) * PIECE)
        both = dot(ws[:, rows], xv[rows, cols], NN)
        return both[0:K] + both[K : 2 * K]

    for n, (lo, hi) in enumerate(CHUNKS):
        if hi - lo < 8:
            mst[n, hi - lo : 8] = jnp.zeros((8 - hi + lo, PIECE), jnp.float32)
            for it in range(ITERS):
                est[it, n, 0, hi - lo : 8] = jnp.zeros((8 - hi + lo, PIECE), jnp.float32)

    load_c.wait()
    offset = split_centroids(0, pl.ds(0, D))
    for it in range(ITERS):
        for n in range(2):
            if it == 0:
                loads[n].wait()
            logits(it, n)
            if it == 0 and n == 0:
                pl.semaphore_wait(barrier, len(peers))
            z_push(it, n, 0)
        macc[...] = jnp.zeros_like(macc)
        for n in range(2):
            z_join(it, n, 0)
            z_push(it, n, 1)
        z_join(it, 0, 1)
        weigh(it, 0)
        for q in range(Q):
            nacc[:, far_cols(q)] = numer(0, far_cols(q))
        for q in range(Q):
            nacc[:, own_cols(q)] = numer(0, own_cols(q))
        z_join(it, 1, 1)
        weigh(it, 1)

        mass = jnp.sum(macc[...], axis=1, keepdims=True)
        eye = lax.broadcasted_iota(jnp.int32, (K, K), 0) == lax.broadcasted_iota(jnp.int32, (K, K), 1)
        mbuf[it, 0] = jnp.sum(jnp.where(eye, mass, 0.0), axis=0, keepdims=True)
        push(mbuf.at[it, 0], mr0.at[it, 0], m_send.at[it, 0], m_recv.at[it, 0], other)

        for q in range(Q):
            nsend[it, q] = nacc[:, far_cols(q)] + numer(1, far_cols(q))
            push(nsend.at[it, q], crecv.at[it, q], c_send.at[it, q], c_recv.at[it, q], other)

        for q in range(Q):
            part = nacc[:, own_cols(q)] + numer(1, own_cols(q))
            await_bytes(crecv.at[it, q], c_recv.at[it, q])
            sbuf[it, q] = part + crecv[it, q]
            for d, (c, device) in enumerate(zip(chips, planes)):
                rows = pl.ds(pl.multiple_of(c * 8, 8), 8)
                push(sbuf.at[it, q, rows], arecv.at[it, q, d], a_send.at[it, q], a_recv.at[it, q], device)
            if q == 0:
                await_bytes(mr0.at[it, 0], m_recv.at[it, 0])
                mbuf[it, 1] = mbuf[it, 0] + mr0[it, 0]
                for d, device in enumerate(planes):
                    push(mbuf.at[it, 1], mr1.at[it, d], m_send.at[it, 1], m_recv.at[it, 1], device)

        await_bytes(mr1.at[it], m_recv.at[it, 1])
        total = mbuf[it, 1] + jnp.sum(mr1[it], axis=0)
        lane = lax.broadcasted_iota(jnp.int32, (8, K), 1)
        want = lax.broadcasted_iota(jnp.int32, (8, K), 0) + base
        denom = jnp.sum(jnp.where(lane == want, total, 0.0), axis=1, keepdims=True) + PRIOR

        for q in range(Q):
            await_bytes(arecv.at[it, q], a_recv.at[it, q])
            got = sbuf[it, q, mine] + jnp.sum(arecv[it, q], axis=0)
            cols = own_cols(q)
            cur[it + 1, mine, cols] = (got + PRIOR * cur[it, mine, cols]) / denom
            block = cur.at[it + 1, mine, cols]
            for device in planes:
                push(block, block, g_send.at[it, q], g_recv.at[it, q], device)
        for q in range(Q):
            await_bytes(cur.at[it + 1, pl.ds(0, 120), own_cols(q)], g_recv.at[it, q])
            block = cur.at[it + 1, :, own_cols(q)]
            push(block, block, gc_send.at[it, q], gc_recv.at[it, q], other)

        if it + 1 < ITERS:
            offset = split_centroids(it + 1, own_half)
            for r0 in range(0, ROWS // PIECE, 2):
                size = min(2, ROWS // PIECE - r0)
                l = product(pl.ds(r0 * PIECE, size * PIECE), own_half)
                for j in range(size):
                    pbuf[r0 + j] = l[:, j * PIECE : (j + 1) * PIECE]
            for q in range(Q):
                await_bytes(cur.at[it + 1, :, far_cols(q)], gc_recv.at[it, q])
            offset = offset + split_centroids(it + 1, far_half)

    last = ITERS
    outs = []

    def store(cols, i):
        copy = pltpu.make_async_copy(cur.at[last, :, cols], out_c.at[:, cols], out_sem.at[i])
        copy.start()
        outs.append(copy)

    for q in range(Q):
        store(own_cols(q), q)
    for n, (lo, hi) in enumerate(CHUNKS):
        out_e[lo:hi] = est[ITERS - 1, n, 2, 0 : hi - lo]
    for q in range(Q):
        await_bytes(cur.at[last, :, far_cols(q)], gc_recv.at[ITERS - 1, q])
        store(far_cols(q), Q + q)

    for it in range(ITERS):
        for n in range(2):
            for stage in range(2):
                await_bytes(zrecv.at[it, n, stage], z_send.at[it, n, stage])
        await_bytes(mr0.at[it, 0], m_send.at[it, 0])
        await_bytes(mr1.at[it], m_send.at[it, 1])
        for q in range(Q):
            await_bytes(crecv.at[it, q], c_send.at[it, q])
            await_bytes(arecv.at[it, q], a_send.at[it, q])
            await_bytes(arecv.at[it, q], g_send.at[it, q])
            await_bytes(crecv.at[it, q], gc_send.at[it, q])
    for copy in outs:
        copy.wait()


def local(embeddings, centroids):
    f32, bf16 = jnp.float32, jnp.bfloat16
    pieces = ROWS // PIECE
    vm = pltpu.VMEM
    dma = pltpu.SemaphoreType.DMA
    new, energy = pl.pallas_call(
        kernel,
        out_shape=(
            jax.ShapeDtypeStruct((K, D), f32),
            jax.ShapeDtypeStruct((pieces, PIECE), f32),
        ),
        in_specs=[pl.BlockSpec(memory_space=pl.ANY)] * 2,
        out_specs=(pl.BlockSpec(memory_space=pl.ANY), pl.BlockSpec(memory_space=pltpu.VMEM)),
        scratch_shapes=[
            vm((ROWS, D), bf16),
            vm((ITERS + 1, K, D), f32),
            vm((2 * K, D), bf16),
            vm((pieces, K, PIECE), f32),
            vm((2 * K, ROWS), bf16),
            vm((K, PIECE), f32),
            vm((2, 8, PIECE), f32),
            vm((ITERS, 2, 3, 8, PIECE), f32),
            vm((ITERS, 2, 2, ZG - 1, 8, PIECE), f32),
            vm((K, D), f32),
            vm((ITERS, Q, K, CW), f32),
            vm((ITERS, Q, K, CW), f32),
            vm((ITERS, Q, K, CW), f32),
            vm((ITERS, Q, N * N - 1, 8, CW), f32),
            vm((ITERS, 2, 1, K), f32),
            vm((ITERS, 1, 1, K), f32),
            vm((ITERS, N * N - 1, 1, K), f32),
            dma((3,)),
            dma((2 * Q,)),
            dma((ITERS, 2, 2)),
            dma((ITERS, 2, 2)),
        ]
        + [dma((ITERS, Q))] * 8
        + [dma((ITERS, 2))] * 2,
        compiler_params=pltpu.CompilerParams(
            collective_id=0, has_side_effects=True, vmem_limit_bytes=53 * 1024 * 1024
        ),
        cost_estimate=pl.CostEstimate(flops=4 * 10**9, bytes_accessed=5 * 10**6, transcendentals=10**6),
    )(embeddings, centroids)
    return new, energy.reshape(ROWS)


def solution(mesh):
    in_specs = (P("dp", None), P("cent", None))
    out_specs = (P("cent", None), P("dp"))
    return jax.shard_map(local, mesh=mesh, in_specs=in_specs, out_specs=out_specs, check_vma=False)
```

```python
import jax
import jax.numpy as jnp
from jax import lax
from jax.experimental import pallas as pl
from jax.experimental.pallas import tpu as pltpu
from jax.sharding import PartitionSpec as P

MESH = pl.DeviceIdType.MESH
ITERS = 2
PRIOR = 2.0
N = 4
PLANE = N * N - 1
Z = 16
ROWS = 1920
D = 1024
K = 128
PIECE = 128
HALF = D // 2
Q = 2
CW = HALF // Q
CHUNKS = ((0, 8), (8, 15))
NT = (((1,), (1,)), ((), ()))
NN = (((1,), (0,)), ((), ()))


def dot(a, b, dims):
    return lax.dot_general(a, b, dims, preferred_element_type=jnp.float32)


def split(v):
    hi = v.astype(jnp.bfloat16)
    lo = (v - hi.astype(jnp.float32)).astype(jnp.bfloat16)
    return hi, lo


def kernel(
    x_hbm, c_hbm, out_c, out_e,
    xv, cur, cs, pbuf, ws, macc, mst, est, energy, zrecv,
    nacc, nbuf, crecv, sbuf, drecv, arecv, mbuf, mrecv,
    ld, z_send, z_recv,
    c_send, c_recv, a_send, a_recv, g_send, g_recv, gc_send, gc_recv, far_recv,
    m_send, m_recv,
):
    dp = lax.axis_index("dp")
    z = lax.axis_index("cent")
    core = lax.rem(dp, 2)
    chip = dp // 2
    cx = lax.rem(chip, N)
    cy = chip // N
    other = (dp + 1 - 2 * core, z)

    def chip_at(dx, dy):
        return lax.rem(cy + dy, N) * N + lax.rem(cx + dx, N)

    moves = [(dx, dy) for dx in range(N) for dy in range(N) if dx or dy]
    moves.sort(key=lambda v: -(min(v[0], N - v[0]) + min(v[1], N - v[1])))
    chips = [chip_at(dx, dy) for dx, dy in moves]
    planes = [(2 * c + core, z) for c in chips]
    cross = [(2 * c + 1 - core, z) for c in chips] + [other]
    places = [pl.ds(pl.multiple_of(c * 8, 8), 8) for c in chips + [chip]]
    along_z = [(dp, lax.rem(z + d, Z)) for d in sorted(range(1, Z), key=lambda d: -min(d, Z - d))]

    def push(src, dst, send, recv, device):
        pltpu.make_async_remote_copy(
            src_ref=src, dst_ref=dst, send_sem=send, recv_sem=recv,
            device_id=device, device_id_type=MESH,
        ).start()

    def await_bytes(ref, sem):
        pltpu.make_async_copy(ref, ref, sem).wait()

    barrier = pltpu.get_barrier_semaphore()
    peers = planes + cross + along_z
    for device in peers:
        pl.semaphore_signal(barrier, inc=1, device_id=device, device_id_type=MESH)

    load_c = pltpu.make_async_copy(c_hbm, cur.at[0], ld.at[0])
    load_c.start()
    loads = []
    for n, (lo, hi) in enumerate(CHUNKS):
        rows = pl.ds(lo * PIECE, (hi - lo) * PIECE)
        loads.append(pltpu.make_async_copy(x_hbm.at[rows], xv.at[rows], ld.at[n + 1]))
        loads[-1].start()

    def own_cols(q):
        return pl.ds(pl.multiple_of(core * HALF + q * CW, CW), CW)

    def far_cols(q):
        return pl.ds(pl.multiple_of((1 - core) * HALF + q * CW, CW), CW)

    far_half = pl.ds(pl.multiple_of((1 - core) * HALF, HALF), HALF)
    base = pl.multiple_of(chip * 8, 8)
    mine = pl.ds(base, 8)

    def split_centroids(it, cols):
        c = cur[it, :, cols]
        hi, lo = split(c)
        cs[0:K, cols] = hi
        cs[K : 2 * K, cols] = lo
        return 0.5 * jnp.sum(c * c, axis=1, keepdims=True)

    def stats(it, n, l, r):
        i = r - CHUNKS[n][0]
        m = jnp.max(l, axis=0, keepdims=True)
        p = jnp.exp(l - m)
        s = jnp.sum(p, axis=0, keepdims=True)
        pbuf[r] = p
        mst[n, i : i + 1] = m
        est[it, n, i : i + 1] = m + jnp.log(s)

    def product(rows, cols):
        both = dot(cs[:, cols], xv[rows, cols], NT)
        return both[0:K] + both[K : 2 * K]

    def logits(it, n):
        lo, hi = CHUNKS[n]
        for r0 in range(lo, hi, 2):
            size = min(2, hi - r0)
            rows = pl.ds(r0 * PIECE, size * PIECE)
            if it == 0:
                l = product(rows, pl.ds(0, D)) - offset
            else:
                l = product(rows, far_half) + product(rows, own_cols(1)) - offset
            for j in range(size):
                part = l[:, j * PIECE : (j + 1) * PIECE]
                stats(it, n, part if it == 0 else part + pbuf[r0 + j], r0 + j)

    def z_push(it, n):
        for device in along_z:
            push(est.at[it, n], zrecv.at[it, n, z], z_send.at[it, n], z_recv.at[it, n], device)
        zrecv[it, n, z] = est[it, n]

    def z_join(it, n):
        await_bytes(zrecv.at[it, n, pl.ds(0, Z - 1)], z_recv.at[it, n])
        e = zrecv[it, n]
        m = jnp.max(e, axis=0)
        energy[it, n] = m + jnp.log(jnp.sum(jnp.exp(e - m[None]), axis=0))

    def weigh(it, n):
        lo, hi = CHUNKS[n]
        f = jnp.exp(mst[n] - energy[it, n])
        for r in range(lo, hi):
            w = pbuf[r] * f[r - lo : r - lo + 1]
            hi_w, lo_w = split(w)
            cols = pl.ds(r * PIECE, PIECE)
            ws[0:K, cols] = hi_w
            ws[K : 2 * K, cols] = lo_w
            macc[...] += w

    def numer(n, cols):
        lo, hi = CHUNKS[n]
        rows = pl.ds(lo * PIECE, (hi - lo) * PIECE)
        both = dot(ws[:, rows], xv[rows, cols], NN)
        return both[0:K] + both[K : 2 * K]

    for n, (lo, hi) in enumerate(CHUNKS):
        if hi - lo < 8:
            mst[n, hi - lo : 8] = jnp.zeros((8 - hi + lo, PIECE), jnp.float32)
            for it in range(ITERS):
                est[it, n, hi - lo : 8] = jnp.zeros((8 - hi + lo, PIECE), jnp.float32)

    load_c.wait()
    offset = split_centroids(0, pl.ds(0, D))
    for it in range(ITERS):
        for n in range(2):
            if it == 0:
                loads[n].wait()
            logits(it, n)
            if it == 0 and n == 0:
                pl.semaphore_wait(barrier, len(peers))
            z_push(it, n)
        macc[...] = jnp.zeros_like(macc)
        z_join(it, 0)
        weigh(it, 0)
        for q in range(Q):
            nacc[:, far_cols(q)] = numer(0, far_cols(q))
        for q in range(Q):
            nacc[:, own_cols(q)] = numer(0, own_cols(q))
        z_join(it, 1)
        weigh(it, 1)

        mass = jnp.sum(macc[...], axis=1, keepdims=True)
        eye = lax.broadcasted_iota(jnp.int32, (K, K), 0) == lax.broadcasted_iota(jnp.int32, (K, K), 1)
        mbuf[it] = jnp.sum(jnp.where(eye, mass, 0.0), axis=0, keepdims=True)

        def total_numer(cols):
            return nacc[:, cols] + numer(1, cols)

        nbuf[it, 2] = total_numer(far_cols(1))
        push(nbuf.at[it, 2], crecv.at[it], c_send.at[it], c_recv.at[it], other)
        nbuf[it, 0] = total_numer(own_cols(0))
        for d, device in enumerate(planes):
            push(nbuf.at[it, 0, places[d]], drecv.at[it, d], a_send.at[it, 0], a_recv.at[it, 0], device)
        nbuf[it, 1] = total_numer(far_cols(0))
        for d, device in enumerate(cross):
            push(nbuf.at[it, 1, places[d]], drecv.at[it, PLANE + d], a_send.at[it, 0], a_recv.at[it, 0], device)
        for d, device in enumerate(planes + cross):
            push(mbuf.at[it], mrecv.at[it, d], m_send.at[it], m_recv.at[it], device)
        part = total_numer(own_cols(1))
        await_bytes(crecv.at[it], c_recv.at[it])
        sbuf[it] = part + crecv[it]
        for d, device in enumerate(planes):
            push(sbuf.at[it, places[d]], arecv.at[it, d], a_send.at[it, 1], a_recv.at[it, 1], device)

        await_bytes(mrecv.at[it], m_recv.at[it])
        total = mbuf[it] + jnp.sum(mrecv[it], axis=0)
        lane = lax.broadcasted_iota(jnp.int32, (8, K), 1)
        want = lax.broadcasted_iota(jnp.int32, (8, K), 0) + base
        denom = jnp.sum(jnp.where(lane == want, total, 0.0), axis=1, keepdims=True) + PRIOR

        fresh = cur.at[it + 1] if it + 1 < ITERS else out_c

        def update(q, got):
            cols = own_cols(q)
            fresh[mine, cols] = (got + PRIOR * cur[it, mine, cols]) / denom
            block = fresh.at[mine, cols]
            for device in planes:
                push(block, block, g_send.at[it, q], g_recv.at[it, q], device)
            return block

        await_bytes(drecv.at[it], a_recv.at[it, 0])
        update(0, nbuf[it, 0, mine] + jnp.sum(drecv[it], axis=0))
        await_bytes(arecv.at[it], a_recv.at[it, 1])
        block = update(1, sbuf[it, mine] + jnp.sum(arecv[it], axis=0))
        for device in cross:
            push(block, block, g_send.at[it, 2], far_recv.at[it], device)

        await_bytes(fresh.at[pl.ds(0, 8 * PLANE), own_cols(0)], g_recv.at[it, 0])
        block = fresh.at[:, own_cols(0)]
        push(block, block, gc_send.at[it], gc_recv.at[it], other)
        if it + 1 < ITERS:
            offset = split_centroids(it + 1, own_cols(0))
            for r0 in range(0, ROWS // PIECE, 2):
                size = min(2, ROWS // PIECE - r0)
                l = product(pl.ds(r0 * PIECE, size * PIECE), own_cols(0))
                for j in range(size):
                    pbuf[r0 + j] = l[:, j * PIECE : (j + 1) * PIECE]
        await_bytes(fresh.at[pl.ds(0, 8 * PLANE), own_cols(1)], g_recv.at[it, 1])
        await_bytes(fresh.at[:, far_cols(1)], far_recv.at[it])
        await_bytes(fresh.at[:, far_cols(0)], gc_recv.at[it])
        if it + 1 < ITERS:
            offset = offset + split_centroids(it + 1, own_cols(1)) + split_centroids(it + 1, far_half)

    for n, (lo, hi) in enumerate(CHUNKS):
        out_e[lo:hi] = energy[ITERS - 1, n, 0 : hi - lo]

    for it in range(ITERS):
        for n in range(2):
            await_bytes(zrecv.at[it, n, pl.ds(0, Z - 1)], z_send.at[it, n])
        await_bytes(mrecv.at[it], m_send.at[it])
        await_bytes(crecv.at[it], c_send.at[it])
        await_bytes(drecv.at[it], a_send.at[it, 0])
        for q in range(Q):
            await_bytes(arecv.at[it], g_send.at[it, q])
        await_bytes(arecv.at[it], a_send.at[it, 1])
        await_bytes(sbuf.at[it, pl.ds(0, 8 * PLANE + 8)], g_send.at[it, 2])
        await_bytes(crecv.at[it], gc_send.at[it])


def local(embeddings, centroids):
    f32, bf16 = jnp.float32, jnp.bfloat16
    pieces = ROWS // PIECE
    vm = pltpu.VMEM
    dma = pltpu.SemaphoreType.DMA
    new, energy = pl.pallas_call(
        kernel,
        out_shape=(
            jax.ShapeDtypeStruct((K, D), f32),
            jax.ShapeDtypeStruct((pieces, PIECE), f32),
        ),
        in_specs=[pl.BlockSpec(memory_space=pl.ANY)] * 2,
        out_specs=(pl.BlockSpec(memory_space=pltpu.VMEM),) * 2,
        scratch_shapes=[
            vm((ROWS, D), bf16),
            vm((ITERS, K, D), f32),
            vm((2 * K, D), bf16),
            vm((pieces, K, PIECE), f32),
            vm((2 * K, ROWS), bf16),
            vm((K, PIECE), f32),
            vm((2, 8, PIECE), f32),
            vm((ITERS, 2, 8, PIECE), f32),
            vm((ITERS, 2, 8, PIECE), f32),
            vm((ITERS, 2, Z, 8, PIECE), f32),
            vm((K, D), f32),
            vm((ITERS, 3, K, CW), f32),
            vm((ITERS, K, CW), f32),
            vm((ITERS, K, CW), f32),
            vm((ITERS, 2 * PLANE + 1, 8, CW), f32),
            vm((ITERS, PLANE, 8, CW), f32),
            vm((ITERS, 1, K), f32),
            vm((ITERS, 2 * PLANE + 1, 1, K), f32),
            dma((3,)),
            dma((ITERS, 2)),
            dma((ITERS, 2)),
        ]
        + [dma((ITERS,))] * 2
        + [dma((ITERS, 2))] * 2
        + [dma((ITERS, 3))] * 2
        + [dma((ITERS,))] * 5,
        compiler_params=pltpu.CompilerParams(
            collective_id=0, has_side_effects=True, vmem_limit_bytes=53 * 1024 * 1024
        ),
        cost_estimate=pl.CostEstimate(flops=4 * 10**9, bytes_accessed=5 * 10**6, transcendentals=10**6),
    )(embeddings, centroids)
    return new, energy.reshape(ROWS)


def solution(mesh):
    in_specs = (P("dp", None), P("cent", None))
    out_specs = (P("cent", None), P("dp"))
    return jax.shard_map(local, mesh=mesh, in_specs=in_specs, out_specs=out_specs, check_vma=False)
```

```python
import jax
import jax.numpy as jnp
from jax import lax
from jax.experimental import pallas as pl
from jax.experimental.pallas import tpu as pltpu
from jax.sharding import PartitionSpec as P

MESH = pl.DeviceIdType.MESH
ITERS = 2
PRIOR = 2.0
N = 4
Z = 16
ROWS = 1920
D = 1024
K = 128
PIECE = 128
HALF = D // 2
Q = 2
CW = HALF // Q
CHUNKS = ((0, 8), (8, 15))
NT = (((1,), (1,)), ((), ()))
NN = (((1,), (0,)), ((), ()))


def dot(a, b, dims):
    return lax.dot_general(a, b, dims, preferred_element_type=jnp.float32)


def split(v):
    hi = v.astype(jnp.bfloat16)
    lo = (v - hi.astype(jnp.float32)).astype(jnp.bfloat16)
    return hi, lo


def kernel(
    x_hbm, c_hbm, out_c, out_e,
    xv, cur, cs, pbuf, ws, macc, mst, est, energy, zrecv,
    nacc, nsend, crecv, sbuf, arecv, mbuf, mr0, mr1,
    ld, z_send, z_recv,
    c_send, c_recv, a_send, a_recv, g_send, g_recv, gc_send, gc_recv,
    m_send, m_recv,
):
    dp = lax.axis_index("dp")
    z = lax.axis_index("cent")
    core = lax.rem(dp, 2)
    chip = dp // 2
    cx = lax.rem(chip, N)
    cy = chip // N
    other = (dp + 1 - 2 * core, z)

    def chip_at(dx, dy):
        return lax.rem(cy + dy, N) * N + lax.rem(cx + dx, N)

    moves = [(dx, dy) for dx in range(N) for dy in range(N) if dx or dy]
    moves.sort(key=lambda v: -(min(v[0], N - v[0]) + min(v[1], N - v[1])))
    chips = [chip_at(dx, dy) for dx, dy in moves]
    planes = [(2 * c + core, z) for c in chips]
    along_z = [(dp, lax.rem(z + d, Z)) for d in sorted(range(1, Z), key=lambda d: -min(d, Z - d))]

    def push(src, dst, send, recv, device):
        pltpu.make_async_remote_copy(
            src_ref=src, dst_ref=dst, send_sem=send, recv_sem=recv,
            device_id=device, device_id_type=MESH,
        ).start()

    def await_bytes(ref, sem):
        pltpu.make_async_copy(ref, ref, sem).wait()

    load_c = pltpu.make_async_copy(c_hbm, cur.at[0], ld.at[0])
    load_c.start()
    loads = []
    for r0 in range(0, ROWS // PIECE, 2):
        rows = pl.ds(r0 * PIECE, min(2, ROWS // PIECE - r0) * PIECE)
        loads.append(pltpu.make_async_copy(x_hbm.at[rows], xv.at[rows], ld.at[1 + r0 // 2]))
        loads[-1].start()

    barrier = pltpu.get_barrier_semaphore()
    peers = [other] + planes + along_z
    for device in peers:
        pl.semaphore_signal(barrier, inc=1, device_id=device, device_id_type=MESH)

    def own_cols(q):
        return pl.ds(pl.multiple_of(core * HALF + q * CW, CW), CW)

    def far_cols(q):
        return pl.ds(pl.multiple_of((1 - core) * HALF + q * CW, CW), CW)

    own_half = pl.ds(pl.multiple_of(core * HALF, HALF), HALF)
    far_half = pl.ds(pl.multiple_of((1 - core) * HALF, HALF), HALF)
    base = pl.multiple_of(chip * 8, 8)
    mine = pl.ds(base, 8)

    def split_centroids(it, cols):
        c = cur[it, :, cols]
        hi, lo = split(c)
        cs[0:K, cols] = hi
        cs[K : 2 * K, cols] = lo
        return 0.5 * jnp.sum(c * c, axis=1, keepdims=True)

    def stats(it, n, l, r):
        i = r - CHUNKS[n][0]
        m = jnp.max(l, axis=0, keepdims=True)
        p = jnp.exp(l - m)
        s = jnp.sum(p, axis=0, keepdims=True)
        pbuf[r] = p
        mst[n, i : i + 1] = m
        est[it, n, i : i + 1] = m + jnp.log(s)

    def product(rows, cols):
        both = dot(cs[:, cols], xv[rows, cols], NT)
        return both[0:K] + both[K : 2 * K]

    def logits(it, n):
        lo, hi = CHUNKS[n]
        for r0 in range(lo, hi, 2):
            size = min(2, hi - r0)
            rows = pl.ds(r0 * PIECE, size * PIECE)
            if it == 0:
                loads[r0 // 2].wait()
            l = product(rows, pl.ds(0, D) if it == 0 else far_half) - offset
            for j in range(size):
                part = l[:, j * PIECE : (j + 1) * PIECE]
                stats(it, n, part if it == 0 else part + pbuf[r0 + j], r0 + j)

    def z_push(it, n):
        for device in along_z:
            push(est.at[it, n], zrecv.at[it, n, z], z_send.at[it, n], z_recv.at[it, n], device)
        zrecv[it, n, z] = est[it, n]

    def z_join(it, n):
        await_bytes(zrecv.at[it, n, pl.ds(0, Z - 1)], z_recv.at[it, n])
        e = zrecv[it, n]
        m = jnp.max(e, axis=0)
        energy[it, n] = m + jnp.log(jnp.sum(jnp.exp(e - m[None]), axis=0))

    def weigh(it, n):
        lo, hi = CHUNKS[n]
        f = jnp.exp(mst[n] - energy[it, n])
        for r in range(lo, hi):
            w = pbuf[r] * f[r - lo : r - lo + 1]
            hi_w, lo_w = split(w)
            cols = pl.ds(r * PIECE, PIECE)
            ws[0:K, cols] = hi_w
            ws[K : 2 * K, cols] = lo_w
            macc[...] += w

    def numer(n, cols):
        lo, hi = CHUNKS[n]
        rows = pl.ds(lo * PIECE, (hi - lo) * PIECE)
        both = dot(ws[:, rows], xv[rows, cols], NN)
        return both[0:K] + both[K : 2 * K]

    for n, (lo, hi) in enumerate(CHUNKS):
        if hi - lo < 8:
            mst[n, hi - lo : 8] = jnp.zeros((8 - hi + lo, PIECE), jnp.float32)
            for it in range(ITERS):
                est[it, n, hi - lo : 8] = jnp.zeros((8 - hi + lo, PIECE), jnp.float32)

    load_c.wait()
    offset = split_centroids(0, pl.ds(0, D))
    for it in range(ITERS):
        for n in range(2):
            logits(it, n)
            if it == 0 and n == 0:
                pl.semaphore_wait(barrier, len(peers))
            z_push(it, n)
        macc[...] = jnp.zeros_like(macc)
        z_join(it, 0)
        weigh(it, 0)
        for q in range(Q):
            nacc[:, far_cols(q)] = numer(0, far_cols(q))
        for q in range(Q):
            nacc[:, own_cols(q)] = numer(0, own_cols(q))
        z_join(it, 1)
        weigh(it, 1)

        mass = jnp.sum(macc[...], axis=1, keepdims=True)
        eye = lax.broadcasted_iota(jnp.int32, (K, K), 0) == lax.broadcasted_iota(jnp.int32, (K, K), 1)
        mbuf[it, 0] = jnp.sum(jnp.where(eye, mass, 0.0), axis=0, keepdims=True)
        push(mbuf.at[it, 0], mr0.at[it, 0], m_send.at[it, 0], m_recv.at[it, 0], other)

        for q in range(Q):
            nsend[it, q] = nacc[:, far_cols(q)] + numer(1, far_cols(q))
            push(nsend.at[it, q], crecv.at[it, q], c_send.at[it, q], c_recv.at[it, q], other)

        for q in range(Q):
            part = nacc[:, own_cols(q)] + numer(1, own_cols(q))
            await_bytes(crecv.at[it, q], c_recv.at[it, q])
            sbuf[it, q] = part + crecv[it, q]
            for d, (c, device) in enumerate(zip(chips, planes)):
                rows = pl.ds(pl.multiple_of(c * 8, 8), 8)
                push(sbuf.at[it, q, rows], arecv.at[it, q, d], a_send.at[it, q], a_recv.at[it, q], device)
            if q == 0:
                await_bytes(mr0.at[it, 0], m_recv.at[it, 0])
                mbuf[it, 1] = mbuf[it, 0] + mr0[it, 0]
                for d, device in enumerate(planes):
                    push(mbuf.at[it, 1], mr1.at[it, d], m_send.at[it, 1], m_recv.at[it, 1], device)

        await_bytes(mr1.at[it], m_recv.at[it, 1])
        total = mbuf[it, 1] + jnp.sum(mr1[it], axis=0)
        lane = lax.broadcasted_iota(jnp.int32, (8, K), 1)
        want = lax.broadcasted_iota(jnp.int32, (8, K), 0) + base
        denom = jnp.sum(jnp.where(lane == want, total, 0.0), axis=1, keepdims=True) + PRIOR

        fresh = cur.at[it + 1] if it + 1 < ITERS else out_c
        for q in range(Q):
            await_bytes(arecv.at[it, q], a_recv.at[it, q])
            got = sbuf[it, q, mine] + jnp.sum(arecv[it, q], axis=0)
            cols = own_cols(q)
            fresh[mine, cols] = (got + PRIOR * cur[it, mine, cols]) / denom
            block = fresh.at[mine, cols]
            for device in planes:
                push(block, block, g_send.at[it, q], g_recv.at[it, q], device)
        for q in range(Q):
            await_bytes(fresh.at[pl.ds(0, 120), own_cols(q)], g_recv.at[it, q])
            block = fresh.at[:, own_cols(q)]
            push(block, block, gc_send.at[it, q], gc_recv.at[it, q], other)

        if it + 1 < ITERS:
            offset = split_centroids(it + 1, own_half)
            for r0 in range(0, ROWS // PIECE, 2):
                size = min(2, ROWS // PIECE - r0)
                l = product(pl.ds(r0 * PIECE, size * PIECE), own_half)
                for j in range(size):
                    pbuf[r0 + j] = l[:, j * PIECE : (j + 1) * PIECE]
            for q in range(Q):
                await_bytes(cur.at[it + 1, :, far_cols(q)], gc_recv.at[it, q])
            offset = offset + split_centroids(it + 1, far_half)

    for n, (lo, hi) in enumerate(CHUNKS):
        out_e[lo:hi] = energy[ITERS - 1, n, 0 : hi - lo]
    for q in range(Q):
        await_bytes(out_c.at[:, far_cols(q)], gc_recv.at[ITERS - 1, q])

    for it in range(ITERS):
        for n in range(2):
            await_bytes(zrecv.at[it, n, pl.ds(0, Z - 1)], z_send.at[it, n])
        await_bytes(mr0.at[it, 0], m_send.at[it, 0])
        await_bytes(mr1.at[it], m_send.at[it, 1])
        for q in range(Q):
            await_bytes(crecv.at[it, q], c_send.at[it, q])
            await_bytes(arecv.at[it, q], a_send.at[it, q])
            await_bytes(arecv.at[it, q], g_send.at[it, q])
            await_bytes(crecv.at[it, q], gc_send.at[it, q])


def local(embeddings, centroids):
    f32, bf16 = jnp.float32, jnp.bfloat16
    pieces = ROWS // PIECE
    vm = pltpu.VMEM
    dma = pltpu.SemaphoreType.DMA
    new, energy = pl.pallas_call(
        kernel,
        out_shape=(
            jax.ShapeDtypeStruct((K, D), f32),
            jax.ShapeDtypeStruct((pieces, PIECE), f32),
        ),
        in_specs=[pl.BlockSpec(memory_space=pl.ANY)] * 2,
        out_specs=(pl.BlockSpec(memory_space=pltpu.VMEM),) * 2,
        scratch_shapes=[
            vm((ROWS, D), bf16),
            vm((ITERS, K, D), f32),
            vm((2 * K, D), bf16),
            vm((pieces, K, PIECE), f32),
            vm((2 * K, ROWS), bf16),
            vm((K, PIECE), f32),
            vm((2, 8, PIECE), f32),
            vm((ITERS, 2, 8, PIECE), f32),
            vm((ITERS, 2, 8, PIECE), f32),
            vm((ITERS, 2, Z, 8, PIECE), f32),
            vm((K, D), f32),
            vm((ITERS, Q, K, CW), f32),
            vm((ITERS, Q, K, CW), f32),
            vm((ITERS, Q, K, CW), f32),
            vm((ITERS, Q, N * N - 1, 8, CW), f32),
            vm((ITERS, 2, 1, K), f32),
            vm((ITERS, 1, 1, K), f32),
            vm((ITERS, N * N - 1, 1, K), f32),
            dma((9,)),
            dma((ITERS, 2)),
            dma((ITERS, 2)),
        ]
        + [dma((ITERS, Q))] * 8
        + [dma((ITERS, 2))] * 2,
        compiler_params=pltpu.CompilerParams(
            collective_id=0, has_side_effects=True, vmem_limit_bytes=53 * 1024 * 1024
        ),
        cost_estimate=pl.CostEstimate(flops=4 * 10**9, bytes_accessed=5 * 10**6, transcendentals=10**6),
    )(embeddings, centroids)
    return new, energy.reshape(ROWS)


def solution(mesh):
    in_specs = (P("dp", None), P("cent", None))
    out_specs = (P("cent", None), P("dp"))
    return jax.shard_map(local, mesh=mesh, in_specs=in_specs, out_specs=out_specs, check_vma=False)
```

```python
import jax
import jax.numpy as jnp
from jax import lax
from jax.experimental import pallas as pl
from jax.experimental.pallas import tpu as pltpu
from jax.sharding import PartitionSpec as P

MESH = pl.DeviceIdType.MESH
ITERS = 2
PRIOR = 2.0
N = 4
Z = 16
ROWS = 1920
D = 1024
K = 128
LANES = 128
PIECE = 128
HALF = D // 2
Q = 2
CW = HALF // Q
CHUNKS = ((0, 8), (8, 15))
NT = (((1,), (1,)), ((), ()))
NN = (((1,), (0,)), ((), ()))


def dot(a, b, dims):
    return lax.dot_general(a, b, dims, preferred_element_type=jnp.float32)


def split(v):
    hi = v.astype(jnp.bfloat16)
    lo = (v - hi.astype(jnp.float32)).astype(jnp.bfloat16)
    return hi, lo


def kernel(
    x_hbm, c_hbm, out_c, out_e,
    nsends, crecvs, sbufs, arecvs,
    xv, cur, cs, pbuf, ws, macc, mst, est, energy, zrecv,
    nacc,
    ld, z_send, z_recv,
    c_send, c_recv, a_send, a_recv, g_send, g_recv, gc_send, gc_recv,
):
    dp = lax.axis_index("dp")
    z = lax.axis_index("cent")
    core = lax.rem(dp, 2)
    chip = dp // 2
    cx = lax.rem(chip, N)
    cy = chip // N
    other = (dp + 1 - 2 * core, z)

    def chip_at(dx, dy):
        return lax.rem(cy + dy, N) * N + lax.rem(cx + dx, N)

    moves = [(dx, dy) for dx in range(N) for dy in range(N) if dx or dy]
    moves.sort(key=lambda v: -(min(v[0], N - v[0]) + min(v[1], N - v[1])))
    chips = [chip_at(dx, dy) for dx, dy in moves]
    planes = [(2 * c + core, z) for c in chips]
    along_z = [(dp, lax.rem(z + d, Z)) for d in sorted(range(1, Z), key=lambda d: -min(d, Z - d))]

    def push(src, dst, send, recv, device):
        pltpu.make_async_remote_copy(
            src_ref=src, dst_ref=dst, send_sem=send, recv_sem=recv,
            device_id=device, device_id_type=MESH,
        ).start()

    def await_bytes(ref, sem):
        pltpu.make_async_copy(ref, ref, sem).wait()

    load_c = pltpu.make_async_copy(c_hbm, cur.at[0], ld.at[0])
    load_c.start()
    loads = []
    for r0 in range(0, ROWS // PIECE, 2):
        rows = pl.ds(r0 * PIECE, min(2, ROWS // PIECE - r0) * PIECE)
        loads.append(pltpu.make_async_copy(x_hbm.at[rows], xv.at[rows], ld.at[1 + r0 // 2]))
        loads[-1].start()

    barrier = pltpu.get_barrier_semaphore()
    peers = [other] + planes + along_z
    for device in peers:
        pl.semaphore_signal(barrier, inc=1, device_id=device, device_id_type=MESH)

    def own_cols(q):
        return pl.ds(pl.multiple_of(core * HALF + q * CW, CW), CW)

    def far_cols(q):
        return pl.ds(pl.multiple_of((1 - core) * HALF + q * CW, CW), CW)

    own_half = pl.ds(pl.multiple_of(core * HALF, HALF), HALF)
    far_half = pl.ds(pl.multiple_of((1 - core) * HALF, HALF), HALF)
    base = pl.multiple_of(chip * 8, 8)
    mine = pl.ds(base, 8)

    def split_centroids(it, cols):
        c = cur[it, :, cols]
        hi, lo = split(c)
        cs[0:K, cols] = hi
        cs[K : 2 * K, cols] = lo
        return 0.5 * jnp.sum(c * c, axis=1, keepdims=True)

    def stats(it, n, l, r):
        i = r - CHUNKS[n][0]
        m = jnp.max(l, axis=0, keepdims=True)
        p = jnp.exp(l - m)
        s = jnp.sum(p, axis=0, keepdims=True)
        pbuf[r] = p
        mst[n, i : i + 1] = m
        est[it, n, i : i + 1] = m + jnp.log(s)

    def product(rows, cols):
        both = dot(cs[:, cols], xv[rows, cols], NT)
        return both[0:K] + both[K : 2 * K]

    def logits(it, n):
        lo, hi = CHUNKS[n]
        for r0 in range(lo, hi, 2):
            size = min(2, hi - r0)
            rows = pl.ds(r0 * PIECE, size * PIECE)
            if it == 0:
                loads[r0 // 2].wait()
            l = product(rows, pl.ds(0, D) if it == 0 else far_half) - offset
            for j in range(size):
                part = l[:, j * PIECE : (j + 1) * PIECE]
                stats(it, n, part if it == 0 else part + pbuf[r0 + j], r0 + j)

    def z_push(it, n):
        for device in along_z:
            push(est.at[it, n], zrecv.at[it, n, z], z_send.at[it, n], z_recv.at[it, n], device)
        zrecv[it, n, z] = est[it, n]

    def z_join(it, n):
        await_bytes(zrecv.at[it, n, pl.ds(0, Z - 1)], z_recv.at[it, n])
        e = zrecv[it, n]
        m = jnp.max(e, axis=0)
        energy[it, n] = m + jnp.log(jnp.sum(jnp.exp(e - m[None]), axis=0))

    def weigh(it, n):
        lo, hi = CHUNKS[n]
        f = jnp.exp(mst[n] - energy[it, n])
        for r in range(lo, hi):
            w = pbuf[r] * f[r - lo : r - lo + 1]
            hi_w, lo_w = split(w)
            cols = pl.ds(r * PIECE, PIECE)
            ws[0:K, cols] = hi_w
            ws[K : 2 * K, cols] = lo_w
            macc[...] += w

    def numer(n, cols):
        lo, hi = CHUNKS[n]
        rows = pl.ds(lo * PIECE, (hi - lo) * PIECE)
        both = dot(ws[:, rows], xv[rows, cols], NN)
        return both[0:K] + both[K : 2 * K]

    for n, (lo, hi) in enumerate(CHUNKS):
        if hi - lo < 8:
            mst[n, hi - lo : 8] = jnp.zeros((8 - hi + lo, PIECE), jnp.float32)
            for it in range(ITERS):
                est[it, n, hi - lo : 8] = jnp.zeros((8 - hi + lo, PIECE), jnp.float32)

    load_c.wait()
    offset = split_centroids(0, pl.ds(0, D))
    for it in range(ITERS):
        for n in range(2):
            logits(it, n)
            if it == 0 and n == 0:
                pl.semaphore_wait(barrier, len(peers))
            z_push(it, n)
        macc[...] = jnp.zeros_like(macc)
        z_join(it, 0)
        weigh(it, 0)
        for q in range(Q):
            nacc[:, far_cols(q)] = numer(0, far_cols(q))
        for q in range(Q):
            nacc[:, own_cols(q)] = numer(0, own_cols(q))
        z_join(it, 1)
        weigh(it, 1)

        mass = jnp.broadcast_to(jnp.sum(macc[...], axis=1, keepdims=True), (K, LANES))

        for q in range(Q):
            nsends[q][it, :, 0:CW] = nacc[:, far_cols(q)] + numer(1, far_cols(q))
            if q == 0:
                nsends[q][it, :, CW:] = mass
            push(nsends[q].at[it], crecvs[q].at[it], c_send.at[it, q], c_recv.at[it, q], other)

        for q in range(Q):
            part = nacc[:, own_cols(q)] + numer(1, own_cols(q))
            await_bytes(crecvs[q].at[it], c_recv.at[it, q])
            sbufs[q][it, :, 0:CW] = part + crecvs[q][it, :, 0:CW]
            if q == 0:
                sbufs[q][it, :, CW:] = mass + crecvs[q][it, :, CW:]
            for d, (c, device) in enumerate(zip(chips, planes)):
                rows = pl.ds(pl.multiple_of(c * 8, 8), 8)
                push(sbufs[q].at[it, rows], arecvs[q].at[it, d], a_send.at[it, q], a_recv.at[it, q], device)

        fresh = cur.at[it + 1] if it + 1 < ITERS else out_c
        for q in range(Q):
            await_bytes(arecvs[q].at[it], a_recv.at[it, q])
            got = sbufs[q][it, mine] + jnp.sum(arecvs[q][it], axis=0)
            if q == 0:
                denom = got[:, CW : CW + 1] + PRIOR
            cols = own_cols(q)
            fresh[mine, cols] = (got[:, 0:CW] + PRIOR * cur[it, mine, cols]) / denom
            block = fresh.at[mine, cols]
            for device in planes:
                push(block, block, g_send.at[it, q], g_recv.at[it, q], device)
        for q in range(Q):
            await_bytes(fresh.at[pl.ds(0, 120), own_cols(q)], g_recv.at[it, q])
            block = fresh.at[:, own_cols(q)]
            push(block, block, gc_send.at[it, q], gc_recv.at[it, q], other)

        if it + 1 < ITERS:
            offset = split_centroids(it + 1, own_half)
            for r0 in range(0, ROWS // PIECE, 2):
                size = min(2, ROWS // PIECE - r0)
                l = product(pl.ds(r0 * PIECE, size * PIECE), own_half)
                for j in range(size):
                    pbuf[r0 + j] = l[:, j * PIECE : (j + 1) * PIECE]
            for q in range(Q):
                await_bytes(cur.at[it + 1, :, far_cols(q)], gc_recv.at[it, q])
            offset = offset + split_centroids(it + 1, far_half)

    for n, (lo, hi) in enumerate(CHUNKS):
        out_e[lo:hi] = energy[ITERS - 1, n, 0 : hi - lo]
    for q in range(Q):
        await_bytes(out_c.at[:, far_cols(q)], gc_recv.at[ITERS - 1, q])

    for it in range(ITERS):
        for n in range(2):
            await_bytes(zrecv.at[it, n, pl.ds(0, Z - 1)], z_send.at[it, n])
        for q in range(Q):
            await_bytes(crecvs[q].at[it], c_send.at[it, q])
            await_bytes(arecvs[q].at[it], a_send.at[it, q])
            await_bytes(arecvs[1].at[it], g_send.at[it, q])
            await_bytes(crecvs[1].at[it], gc_send.at[it, q])


def local(embeddings, centroids):
    f32, bf16 = jnp.float32, jnp.bfloat16
    pieces = ROWS // PIECE
    widths = (CW + LANES, CW)
    vm = pltpu.VMEM
    dma = pltpu.SemaphoreType.DMA
    new, energy = pl.pallas_call(
        kernel,
        out_shape=(
            jax.ShapeDtypeStruct((K, D), f32),
            jax.ShapeDtypeStruct((pieces, PIECE), f32),
        ),
        in_specs=[pl.BlockSpec(memory_space=pl.ANY)] * 2,
        out_specs=(pl.BlockSpec(memory_space=pltpu.VMEM),) * 2,
        scratch_shapes=[
            [vm((ITERS, K, v), f32) for v in widths],
            [vm((ITERS, K, v), f32) for v in widths],
            [vm((ITERS, K, v), f32) for v in widths],
            [vm((ITERS, N * N - 1, 8, v), f32) for v in widths],
            vm((ROWS, D), bf16),
            vm((ITERS, K, D), f32),
            vm((2 * K, D), bf16),
            vm((pieces, K, PIECE), f32),
            vm((2 * K, ROWS), bf16),
            vm((K, PIECE), f32),
            vm((2, 8, PIECE), f32),
            vm((ITERS, 2, 8, PIECE), f32),
            vm((ITERS, 2, 8, PIECE), f32),
            vm((ITERS, 2, Z, 8, PIECE), f32),
            vm((K, D), f32),
            dma((9,)),
            dma((ITERS, 2)),
            dma((ITERS, 2)),
        ]
        + [dma((ITERS, Q))] * 8,
        compiler_params=pltpu.CompilerParams(
            collective_id=0, has_side_effects=True, vmem_limit_bytes=53 * 1024 * 1024
        ),
        cost_estimate=pl.CostEstimate(flops=4 * 10**9, bytes_accessed=5 * 10**6, transcendentals=10**6),
    )(embeddings, centroids)
    return new, energy.reshape(ROWS)


def solution(mesh):
    in_specs = (P("dp", None), P("cent", None))
    out_specs = (P("cent", None), P("dp"))
    return jax.shard_map(local, mesh=mesh, in_specs=in_specs, out_specs=out_specs, check_vma=False)
```

```python
import jax
import jax.numpy as jnp
from jax import lax
from jax.experimental import pallas as pl
from jax.experimental.pallas import tpu as pltpu
from jax.sharding import PartitionSpec as P

MESH = pl.DeviceIdType.MESH
ITERS = 2
PRIOR = 2.0
N = 4
Z = 16
ROWS = 1920
D = 1024
K = 128
PIECE = 128
HALF = D // 2
Q = 2
CW = HALF // Q
CHUNKS = ((0, 8), (8, 15))
NT = (((1,), (1,)), ((), ()))
NN = (((1,), (0,)), ((), ()))


def dot(a, b, dims):
    return lax.dot_general(a, b, dims, preferred_element_type=jnp.float32)


def split(v):
    hi = v.astype(jnp.bfloat16)
    lo = (v - hi.astype(jnp.float32)).astype(jnp.bfloat16)
    return hi, lo


def kernel(
    x_hbm, c_hbm, out_c, out_e,
    msts, ests, energies, zrecvs,
    xv, cur, cs, pbuf, ws, macc,
    nacc, nsend, crecv, sbuf, arecv, mbuf, mr0, mr1,
    ld, z_send, z_recv,
    c_send, c_recv, a_send, a_recv, g_send, g_recv, gc_send, gc_recv,
    m_send, m_recv,
):
    dp = lax.axis_index("dp")
    z = lax.axis_index("cent")
    core = lax.rem(dp, 2)
    chip = dp // 2
    cx = lax.rem(chip, N)
    cy = chip // N
    other = (dp + 1 - 2 * core, z)

    def chip_at(dx, dy):
        return lax.rem(cy + dy, N) * N + lax.rem(cx + dx, N)

    moves = [(dx, dy) for dx in range(N) for dy in range(N) if dx or dy]
    moves.sort(key=lambda v: -(min(v[0], N - v[0]) + min(v[1], N - v[1])))
    chips = [chip_at(dx, dy) for dx, dy in moves]
    planes = [(2 * c + core, z) for c in chips]
    along_z = [(dp, lax.rem(z + d, Z)) for d in sorted(range(1, Z), key=lambda d: -min(d, Z - d))]

    def push(src, dst, send, recv, device):
        pltpu.make_async_remote_copy(
            src_ref=src, dst_ref=dst, send_sem=send, recv_sem=recv,
            device_id=device, device_id_type=MESH,
        ).start()

    def await_bytes(ref, sem):
        pltpu.make_async_copy(ref, ref, sem).wait()

    load_c = pltpu.make_async_copy(c_hbm, cur.at[0], ld.at[0])
    load_c.start()
    loads = []
    for r0 in range(0, ROWS // PIECE, 2):
        rows = pl.ds(r0 * PIECE, min(2, ROWS // PIECE - r0) * PIECE)
        loads.append(pltpu.make_async_copy(x_hbm.at[rows], xv.at[rows], ld.at[1 + r0 // 2]))
        loads[-1].start()

    barrier = pltpu.get_barrier_semaphore()
    peers = [other] + planes + along_z
    for device in peers:
        pl.semaphore_signal(barrier, inc=1, device_id=device, device_id_type=MESH)

    def own_cols(q):
        return pl.ds(pl.multiple_of(core * HALF + q * CW, CW), CW)

    def far_cols(q):
        return pl.ds(pl.multiple_of((1 - core) * HALF + q * CW, CW), CW)

    own_half = pl.ds(pl.multiple_of(core * HALF, HALF), HALF)
    far_half = pl.ds(pl.multiple_of((1 - core) * HALF, HALF), HALF)
    base = pl.multiple_of(chip * 8, 8)
    mine = pl.ds(base, 8)

    def split_centroids(it, cols):
        c = cur[it, :, cols]
        hi, lo = split(c)
        cs[0:K, cols] = hi
        cs[K : 2 * K, cols] = lo
        return 0.5 * jnp.sum(c * c, axis=1, keepdims=True)

    def stats(it, n, l, r):
        i = r - CHUNKS[n][0]
        m = jnp.max(l, axis=0, keepdims=True)
        p = jnp.exp(l - m)
        s = jnp.sum(p, axis=0, keepdims=True)
        pbuf[r] = p
        msts[n][i : i + 1] = m
        ests[n][it, i : i + 1] = m + jnp.log(s)

    def product(rows, cols):
        both = dot(cs[:, cols], xv[rows, cols], NT)
        return both[0:K] + both[K : 2 * K]

    def logits(it, n):
        lo, hi = CHUNKS[n]
        for r0 in range(lo, hi, 2):
            size = min(2, hi - r0)
            rows = pl.ds(r0 * PIECE, size * PIECE)
            if it == 0:
                loads[r0 // 2].wait()
            l = product(rows, pl.ds(0, D) if it == 0 else far_half) - offset
            for j in range(size):
                part = l[:, j * PIECE : (j + 1) * PIECE]
                stats(it, n, part if it == 0 else part + pbuf[r0 + j], r0 + j)

    def z_push(it, n):
        for device in along_z:
            push(ests[n].at[it], zrecvs[n].at[it, z], z_send.at[it, n], z_recv.at[it, n], device)
        zrecvs[n][it, z] = ests[n][it]

    def z_join(it, n):
        await_bytes(zrecvs[n].at[it, pl.ds(0, Z - 1)], z_recv.at[it, n])
        e = zrecvs[n][it]
        m = jnp.max(e, axis=0)
        energies[n][it] = m + jnp.log(jnp.sum(jnp.exp(e - m[None]), axis=0))

    def weigh(it, n):
        lo, hi = CHUNKS[n]
        f = jnp.exp(msts[n][...] - energies[n][it])
        for r in range(lo, hi):
            w = pbuf[r] * f[r - lo : r - lo + 1]
            hi_w, lo_w = split(w)
            cols = pl.ds(r * PIECE, PIECE)
            ws[0:K, cols] = hi_w
            ws[K : 2 * K, cols] = lo_w
            macc[...] += w

    def numer(n, cols):
        lo, hi = CHUNKS[n]
        rows = pl.ds(lo * PIECE, (hi - lo) * PIECE)
        both = dot(ws[:, rows], xv[rows, cols], NN)
        return both[0:K] + both[K : 2 * K]

    load_c.wait()
    offset = split_centroids(0, pl.ds(0, D))
    for it in range(ITERS):
        for n in range(2):
            logits(it, n)
            if it == 0 and n == 0:
                pl.semaphore_wait(barrier, len(peers))
            z_push(it, n)
        macc[...] = jnp.zeros_like(macc)
        z_join(it, 0)
        weigh(it, 0)
        for q in range(Q):
            nacc[:, far_cols(q)] = numer(0, far_cols(q))
        for q in range(Q):
            nacc[:, own_cols(q)] = numer(0, own_cols(q))
        z_join(it, 1)
        weigh(it, 1)

        mass = jnp.sum(macc[...], axis=1, keepdims=True)
        eye = lax.broadcasted_iota(jnp.int32, (K, K), 0) == lax.broadcasted_iota(jnp.int32, (K, K), 1)
        mbuf[it, 0] = jnp.sum(jnp.where(eye, mass, 0.0), axis=0, keepdims=True)
        push(mbuf.at[it, 0], mr0.at[it, 0], m_send.at[it, 0], m_recv.at[it, 0], other)

        for q in range(Q):
            nsend[it, q] = nacc[:, far_cols(q)] + numer(1, far_cols(q))
            push(nsend.at[it, q], crecv.at[it, q], c_send.at[it, q], c_recv.at[it, q], other)

        for q in range(Q):
            part = nacc[:, own_cols(q)] + numer(1, own_cols(q))
            if q == 0:
                await_bytes(mr0.at[it, 0], m_recv.at[it, 0])
                mbuf[it, 1] = mbuf[it, 0] + mr0[it, 0]
                for d, device in enumerate(planes):
                    push(mbuf.at[it, 1], mr1.at[it, d], m_send.at[it, 1], m_recv.at[it, 1], device)
            await_bytes(crecv.at[it, q], c_recv.at[it, q])
            sbuf[it, q] = part + crecv[it, q]
            for d, (c, device) in enumerate(zip(chips, planes)):
                rows = pl.ds(pl.multiple_of(c * 8, 8), 8)
                push(sbuf.at[it, q, rows], arecv.at[it, q, d], a_send.at[it, q], a_recv.at[it, q], device)

        await_bytes(mr1.at[it], m_recv.at[it, 1])
        total = mbuf[it, 1] + jnp.sum(mr1[it], axis=0)
        lane = lax.broadcasted_iota(jnp.int32, (8, K), 1)
        want = lax.broadcasted_iota(jnp.int32, (8, K), 0) + base
        denom = jnp.sum(jnp.where(lane == want, total, 0.0), axis=1, keepdims=True) + PRIOR

        fresh = cur.at[it + 1] if it + 1 < ITERS else out_c
        for q in range(Q):
            await_bytes(arecv.at[it, q], a_recv.at[it, q])
            got = sbuf[it, q, mine] + jnp.sum(arecv[it, q], axis=0)
            cols = own_cols(q)
            fresh[mine, cols] = (got + PRIOR * cur[it, mine, cols]) / denom
            block = fresh.at[mine, cols]
            for device in planes:
                push(block, block, g_send.at[it, q], g_recv.at[it, q], device)
        for q in range(Q):
            await_bytes(fresh.at[pl.ds(0, 120), own_cols(q)], g_recv.at[it, q])
            block = fresh.at[:, own_cols(q)]
            push(block, block, gc_send.at[it, q], gc_recv.at[it, q], other)

        if it + 1 < ITERS:
            offset = split_centroids(it + 1, own_half)
            for r0 in range(0, ROWS // PIECE, 2):
                size = min(2, ROWS // PIECE - r0)
                l = product(pl.ds(r0 * PIECE, size * PIECE), own_half)
                for j in range(size):
                    pbuf[r0 + j] = l[:, j * PIECE : (j + 1) * PIECE]
            for q in range(Q):
                await_bytes(cur.at[it + 1, :, far_cols(q)], gc_recv.at[it, q])
            offset = offset + split_centroids(it + 1, far_half)

    for n, (lo, hi) in enumerate(CHUNKS):
        out_e[lo:hi] = energies[n][ITERS - 1]
    for q in range(Q):
        await_bytes(out_c.at[:, far_cols(q)], gc_recv.at[ITERS - 1, q])

    for it in range(ITERS):
        for n in range(2):
            await_bytes(zrecvs[n].at[it, pl.ds(0, Z - 1)], z_send.at[it, n])
        await_bytes(mr0.at[it, 0], m_send.at[it, 0])
        await_bytes(mr1.at[it], m_send.at[it, 1])
        for q in range(Q):
            await_bytes(crecv.at[it, q], c_send.at[it, q])
            await_bytes(arecv.at[it, q], a_send.at[it, q])
            await_bytes(arecv.at[it, q], g_send.at[it, q])
            await_bytes(crecv.at[it, q], gc_send.at[it, q])


def local(embeddings, centroids):
    f32, bf16 = jnp.float32, jnp.bfloat16
    pieces = ROWS // PIECE
    sizes = [hi - lo for lo, hi in CHUNKS]
    vm = pltpu.VMEM
    dma = pltpu.SemaphoreType.DMA
    new, energy = pl.pallas_call(
        kernel,
        out_shape=(
            jax.ShapeDtypeStruct((K, D), f32),
            jax.ShapeDtypeStruct((pieces, PIECE), f32),
        ),
        in_specs=[pl.BlockSpec(memory_space=pl.ANY)] * 2,
        out_specs=(pl.BlockSpec(memory_space=pltpu.VMEM),) * 2,
        scratch_shapes=[
            [vm((v, PIECE), f32) for v in sizes],
            [vm((ITERS, v, PIECE), f32) for v in sizes],
            [vm((ITERS, v, PIECE), f32) for v in sizes],
            [vm((ITERS, Z, v, PIECE), f32) for v in sizes],
            vm((ROWS, D), bf16),
            vm((ITERS, K, D), f32),
            vm((2 * K, D), bf16),
            vm((pieces, K, PIECE), f32),
            vm((2 * K, ROWS), bf16),
            vm((K, PIECE), f32),
            vm((K, D), f32),
            vm((ITERS, Q, K, CW), f32),
            vm((ITERS, Q, K, CW), f32),
            vm((ITERS, Q, K, CW), f32),
            vm((ITERS, Q, N * N - 1, 8, CW), f32),
            vm((ITERS, 2, 1, K), f32),
            vm((ITERS, 1, 1, K), f32),
            vm((ITERS, N * N - 1, 1, K), f32),
            dma((9,)),
            dma((ITERS, 2)),
            dma((ITERS, 2)),
        ]
        + [dma((ITERS, Q))] * 8
        + [dma((ITERS, 2))] * 2,
        compiler_params=pltpu.CompilerParams(
            collective_id=0, has_side_effects=True, vmem_limit_bytes=53 * 1024 * 1024
        ),
        cost_estimate=pl.CostEstimate(flops=4 * 10**9, bytes_accessed=5 * 10**6, transcendentals=10**6),
    )(embeddings, centroids)
    return new, energy.reshape(ROWS)


def solution(mesh):
    in_specs = (P("dp", None), P("cent", None))
    out_specs = (P("cent", None), P("dp"))
    return jax.shard_map(local, mesh=mesh, in_specs=in_specs, out_specs=out_specs, check_vma=False)
```

```python
import jax
import jax.numpy as jnp
from jax import lax
from jax.experimental import pallas as pl
from jax.experimental.pallas import tpu as pltpu
from jax.sharding import PartitionSpec as P

MESH = pl.DeviceIdType.MESH
ITERS = 2
PRIOR = 2.0
N = 4
Z = 16
ROWS = 1920
D = 1024
K = 128
PIECE = 128
HALF = D // 2
Q = 2
CW = HALF // Q
CHUNKS = ((0, 8), (8, 15))
NT = (((1,), (1,)), ((), ()))
NN = (((1,), (0,)), ((), ()))


def dot(a, b, dims):
    return lax.dot_general(a, b, dims, preferred_element_type=jnp.float32)


def split(v):
    hi = v.astype(jnp.bfloat16)
    lo = (v - hi.astype(jnp.float32)).astype(jnp.bfloat16)
    return hi, lo


def kernel(
    x_hbm, c_hbm, out_c, out_e,
    msts, ests, energies, zrecvs,
    xv, cur, cs, pbuf, ws, macc,
    nacc, nsend, crecv, sbuf, arecv, mbuf, mr0, mr1,
    ld, z_send, z_recv,
    c_send, c_recv, a_send, a_recv, g_send, g_recv, gc_send, gc_recv,
    m_send, m_recv,
):
    dp = lax.axis_index("dp")
    z = lax.axis_index("cent")
    core = lax.rem(dp, 2)
    chip = dp // 2
    cx = lax.rem(chip, N)
    cy = chip // N
    other = (dp + 1 - 2 * core, z)

    def chip_at(dx, dy):
        return lax.rem(cy + dy, N) * N + lax.rem(cx + dx, N)

    def plane_chip(d):
        return chip_at(lax.rem(d, N), d // N)

    def along_z(d):
        return (dp, lax.rem(z + d, Z))

    def push(src, dst, send, recv, device):
        pltpu.make_async_remote_copy(
            src_ref=src, dst_ref=dst, send_sem=send, recv_sem=recv,
            device_id=device, device_id_type=MESH,
        ).start()

    def await_bytes(ref, sem):
        pltpu.make_async_copy(ref, ref, sem).wait()

    load_c = pltpu.make_async_copy(c_hbm, cur.at[0], ld.at[0])
    load_c.start()
    loads = []
    for r0 in range(0, ROWS // PIECE, 2):
        rows = pl.ds(r0 * PIECE, min(2, ROWS // PIECE - r0) * PIECE)
        loads.append(pltpu.make_async_copy(x_hbm.at[rows], xv.at[rows], ld.at[1 + r0 // 2]))
        loads[-1].start()

    barrier = pltpu.get_barrier_semaphore()

    def greet(device):
        pl.semaphore_signal(barrier, inc=1, device_id=device, device_id_type=MESH)

    greet(other)

    @pl.loop(1, N * N)
    def _(d):
        greet((2 * plane_chip(d) + core, z))
        greet(along_z(d))

    def own_cols(q):
        return pl.ds(pl.multiple_of(core * HALF + q * CW, CW), CW)

    def far_cols(q):
        return pl.ds(pl.multiple_of((1 - core) * HALF + q * CW, CW), CW)

    own_half = pl.ds(pl.multiple_of(core * HALF, HALF), HALF)
    far_half = pl.ds(pl.multiple_of((1 - core) * HALF, HALF), HALF)
    base = pl.multiple_of(chip * 8, 8)
    mine = pl.ds(base, 8)

    def split_centroids(it, cols):
        c = cur[it, :, cols]
        hi, lo = split(c)
        cs[0:K, cols] = hi
        cs[K : 2 * K, cols] = lo
        return 0.5 * jnp.sum(c * c, axis=1, keepdims=True)

    def stats(it, n, l, r):
        i = r - CHUNKS[n][0]
        m = jnp.max(l, axis=0, keepdims=True)
        p = jnp.exp(l - m)
        s = jnp.sum(p, axis=0, keepdims=True)
        pbuf[r] = p
        msts[n][i : i + 1] = m
        ests[n][it, i : i + 1] = m + jnp.log(s)

    def product(rows, cols):
        both = dot(cs[:, cols], xv[rows, cols], NT)
        return both[0:K] + both[K : 2 * K]

    def logits(it, n):
        lo, hi = CHUNKS[n]
        for r0 in range(lo, hi, 2):
            size = min(2, hi - r0)
            rows = pl.ds(r0 * PIECE, size * PIECE)
            if it == 0:
                loads[r0 // 2].wait()
            l = product(rows, pl.ds(0, D) if it == 0 else far_half) - offset
            for j in range(size):
                part = l[:, j * PIECE : (j + 1) * PIECE]
                stats(it, n, part if it == 0 else part + pbuf[r0 + j], r0 + j)

    def z_push(it, n):
        @pl.loop(1, Z)
        def _(d):
            push(ests[n].at[it], zrecvs[n].at[it, z], z_send.at[it, n], z_recv.at[it, n], along_z(d))

        zrecvs[n][it, z] = ests[n][it]

    def z_join(it, n):
        await_bytes(zrecvs[n].at[it, pl.ds(0, Z - 1)], z_recv.at[it, n])
        e = zrecvs[n][it]
        m = jnp.max(e, axis=0)
        energies[n][it] = m + jnp.log(jnp.sum(jnp.exp(e - m[None]), axis=0))

    def weigh(it, n):
        lo, hi = CHUNKS[n]
        f = jnp.exp(msts[n][...] - energies[n][it])
        for r in range(lo, hi):
            w = pbuf[r] * f[r - lo : r - lo + 1]
            hi_w, lo_w = split(w)
            cols = pl.ds(r * PIECE, PIECE)
            ws[0:K, cols] = hi_w
            ws[K : 2 * K, cols] = lo_w
            macc[...] += w

    def numer(n, cols):
        lo, hi = CHUNKS[n]
        rows = pl.ds(lo * PIECE, (hi - lo) * PIECE)
        both = dot(ws[:, rows], xv[rows, cols], NN)
        return both[0:K] + both[K : 2 * K]

    load_c.wait()
    offset = split_centroids(0, pl.ds(0, D))
    for it in range(ITERS):
        for n in range(2):
            logits(it, n)
            if it == 0 and n == 0:
                pl.semaphore_wait(barrier, N * N - 1 + Z)
            z_push(it, n)
        macc[...] = jnp.zeros_like(macc)
        z_join(it, 0)
        weigh(it, 0)
        for q in range(Q):
            nacc[:, far_cols(q)] = numer(0, far_cols(q))
        for q in range(Q):
            nacc[:, own_cols(q)] = numer(0, own_cols(q))
        z_join(it, 1)
        weigh(it, 1)

        mass = jnp.sum(macc[...], axis=1, keepdims=True)
        eye = lax.broadcasted_iota(jnp.int32, (K, K), 0) == lax.broadcasted_iota(jnp.int32, (K, K), 1)
        mbuf[it, 0] = jnp.sum(jnp.where(eye, mass, 0.0), axis=0, keepdims=True)
        push(mbuf.at[it, 0], mr0.at[it, 0], m_send.at[it, 0], m_recv.at[it, 0], other)

        for q in range(Q):
            nsend[it, q] = nacc[:, far_cols(q)] + numer(1, far_cols(q))
            push(nsend.at[it, q], crecv.at[it, q], c_send.at[it, q], c_recv.at[it, q], other)

        for q in range(Q):
            part = nacc[:, own_cols(q)] + numer(1, own_cols(q))
            if q == 0:
                await_bytes(mr0.at[it, 0], m_recv.at[it, 0])
                mbuf[it, 1] = mbuf[it, 0] + mr0[it, 0]

                @pl.loop(1, N * N)
                def _(d):
                    device = (2 * plane_chip(d) + core, z)
                    push(mbuf.at[it, 1], mr1.at[it, d - 1], m_send.at[it, 1], m_recv.at[it, 1], device)

            await_bytes(crecv.at[it, q], c_recv.at[it, q])
            sbuf[it, q] = part + crecv[it, q]

            @pl.loop(1, N * N)
            def _(d):
                c = plane_chip(d)
                rows = pl.ds(pl.multiple_of(c * 8, 8), 8)
                push(sbuf.at[it, q, rows], arecv.at[it, q, d - 1], a_send.at[it, q], a_recv.at[it, q], (2 * c + core, z))


        await_bytes(mr1.at[it], m_recv.at[it, 1])
        total = mbuf[it, 1] + jnp.sum(mr1[it], axis=0)
        lane = lax.broadcasted_iota(jnp.int32, (8, K), 1)
        want = lax.broadcasted_iota(jnp.int32, (8, K), 0) + base
        denom = jnp.sum(jnp.where(lane == want, total, 0.0), axis=1, keepdims=True) + PRIOR

        fresh = cur.at[it + 1] if it + 1 < ITERS else out_c
        for q in range(Q):
            await_bytes(arecv.at[it, q], a_recv.at[it, q])
            got = sbuf[it, q, mine] + jnp.sum(arecv[it, q], axis=0)
            cols = own_cols(q)
            fresh[mine, cols] = (got + PRIOR * cur[it, mine, cols]) / denom
            block = fresh.at[mine, cols]

            @pl.loop(1, N * N)
            def _(d):
                push(block, block, g_send.at[it, q], g_recv.at[it, q], (2 * plane_chip(d) + core, z))

        for q in range(Q):
            await_bytes(fresh.at[pl.ds(0, 120), own_cols(q)], g_recv.at[it, q])
            block = fresh.at[:, own_cols(q)]
            push(block, block, gc_send.at[it, q], gc_recv.at[it, q], other)

        if it + 1 < ITERS:
            offset = split_centroids(it + 1, own_half)
            for r0 in range(0, ROWS // PIECE, 2):
                size = min(2, ROWS // PIECE - r0)
                l = product(pl.ds(r0 * PIECE, size * PIECE), own_half)
                for j in range(size):
                    pbuf[r0 + j] = l[:, j * PIECE : (j + 1) * PIECE]
            for q in range(Q):
                await_bytes(cur.at[it + 1, :, far_cols(q)], gc_recv.at[it, q])
            offset = offset + split_centroids(it + 1, far_half)

    for n, (lo, hi) in enumerate(CHUNKS):
        out_e[lo:hi] = energies[n][ITERS - 1]
    for q in range(Q):
        await_bytes(out_c.at[:, far_cols(q)], gc_recv.at[ITERS - 1, q])

    for it in range(ITERS):
        for n in range(2):
            await_bytes(zrecvs[n].at[it, pl.ds(0, Z - 1)], z_send.at[it, n])
        await_bytes(mr0.at[it, 0], m_send.at[it, 0])
        await_bytes(mr1.at[it], m_send.at[it, 1])
        for q in range(Q):
            await_bytes(crecv.at[it, q], c_send.at[it, q])
            await_bytes(arecv.at[it, q], a_send.at[it, q])
            await_bytes(arecv.at[it, q], g_send.at[it, q])
            await_bytes(crecv.at[it, q], gc_send.at[it, q])


def local(embeddings, centroids):
    f32, bf16 = jnp.float32, jnp.bfloat16
    pieces = ROWS // PIECE
    sizes = [hi - lo for lo, hi in CHUNKS]
    vm = pltpu.VMEM
    dma = pltpu.SemaphoreType.DMA
    new, energy = pl.pallas_call(
        kernel,
        out_shape=(
            jax.ShapeDtypeStruct((K, D), f32),
            jax.ShapeDtypeStruct((pieces, PIECE), f32),
        ),
        in_specs=[pl.BlockSpec(memory_space=pl.ANY)] * 2,
        out_specs=(pl.BlockSpec(memory_space=pltpu.VMEM),) * 2,
        scratch_shapes=[
            [vm((v, PIECE), f32) for v in sizes],
            [vm((ITERS, v, PIECE), f32) for v in sizes],
            [vm((ITERS, v, PIECE), f32) for v in sizes],
            [vm((ITERS, Z, v, PIECE), f32) for v in sizes],
            vm((ROWS, D), bf16),
            vm((ITERS, K, D), f32),
            vm((2 * K, D), bf16),
            vm((pieces, K, PIECE), f32),
            vm((2 * K, ROWS), bf16),
            vm((K, PIECE), f32),
            vm((K, D), f32),
            vm((ITERS, Q, K, CW), f32),
            vm((ITERS, Q, K, CW), f32),
            vm((ITERS, Q, K, CW), f32),
            vm((ITERS, Q, N * N - 1, 8, CW), f32),
            vm((ITERS, 2, 1, K), f32),
            vm((ITERS, 1, 1, K), f32),
            vm((ITERS, N * N - 1, 1, K), f32),
            dma((9,)),
            dma((ITERS, 2)),
            dma((ITERS, 2)),
        ]
        + [dma((ITERS, Q))] * 8
        + [dma((ITERS, 2))] * 2,
        compiler_params=pltpu.CompilerParams(
            collective_id=0, has_side_effects=True, vmem_limit_bytes=53 * 1024 * 1024
        ),
        cost_estimate=pl.CostEstimate(flops=4 * 10**9, bytes_accessed=5 * 10**6, transcendentals=10**6),
    )(embeddings, centroids)
    return new, energy.reshape(ROWS)


def solution(mesh):
    in_specs = (P("dp", None), P("cent", None))
    out_specs = (P("cent", None), P("dp"))
    return jax.shard_map(local, mesh=mesh, in_specs=in_specs, out_specs=out_specs, check_vma=False)
```

```python
import jax
import jax.numpy as jnp
from jax import lax
from jax.experimental import pallas as pl
from jax.experimental.pallas import tpu as pltpu
from jax.sharding import PartitionSpec as P

MESH = pl.DeviceIdType.MESH
ITERS = 2
PRIOR = 2.0
N = 4
Z = 16
ROWS = 1920
D = 1024
K = 128
PIECE = 128
HALF = D // 2
Q = 2
CW = HALF // Q
CHUNKS = ((0, 8), (8, 15))
NT = (((1,), (1,)), ((), ()))
NN = (((1,), (0,)), ((), ()))


def dot(a, b, dims):
    return lax.dot_general(a, b, dims, preferred_element_type=jnp.float32)


def split(v):
    hi = v.astype(jnp.bfloat16)
    lo = (v - hi.astype(jnp.float32)).astype(jnp.bfloat16)
    return hi, lo


def kernel(
    x_hbm, c_hbm, out_c, out_e,
    msts, ests, energies, zrecvs,
    xv, cur, cs, pbuf, ws, macc,
    nacc, nsend, crecv, sbuf, arecv, mbuf, mr0, mr1,
    ld, z_send, z_recv,
    c_send, c_recv, a_send, a_recv, g_send, g_recv, gc_send, gc_recv,
    m_send, m_recv,
):
    dp = lax.axis_index("dp")
    z = lax.axis_index("cent")
    core = lax.rem(dp, 2)
    chip = dp // 2
    cx = lax.rem(chip, N)
    cy = chip // N
    other = (dp + 1 - 2 * core, z)

    def chip_at(dx, dy):
        return lax.rem(cy + dy, N) * N + lax.rem(cx + dx, N)

    moves = [(dx, dy) for dx in range(N) for dy in range(N) if dx or dy]
    moves.sort(key=lambda v: -(min(v[0], N - v[0]) + min(v[1], N - v[1])))
    chips = [chip_at(dx, dy) for dx, dy in moves]
    planes = [(2 * c + core, z) for c in chips]
    along_z = [(dp, lax.rem(z + d, Z)) for d in sorted(range(1, Z), key=lambda d: -min(d, Z - d))]

    def push(src, dst, send, recv, device):
        pltpu.make_async_remote_copy(
            src_ref=src, dst_ref=dst, send_sem=send, recv_sem=recv,
            device_id=device, device_id_type=MESH,
        ).start()

    def await_bytes(ref, sem):
        pltpu.make_async_copy(ref, ref, sem).wait()

    load_c = pltpu.make_async_copy(c_hbm, cur.at[0], ld.at[0])
    load_c.start()
    loads = []
    for r0 in range(0, ROWS // PIECE, 2):
        rows = pl.ds(r0 * PIECE, min(2, ROWS // PIECE - r0) * PIECE)
        loads.append(pltpu.make_async_copy(x_hbm.at[rows], xv.at[rows], ld.at[1 + r0 // 2]))
        loads[-1].start()

    barrier = pltpu.get_barrier_semaphore()
    peers = [other] + planes + along_z
    for device in peers:
        pl.semaphore_signal(barrier, inc=1, device_id=device, device_id_type=MESH)

    def own_cols(q):
        return pl.ds(pl.multiple_of(core * HALF + q * CW, CW), CW)

    def far_cols(q):
        return pl.ds(pl.multiple_of((1 - core) * HALF + q * CW, CW), CW)

    base = pl.multiple_of(chip * 8, 8)
    mine = pl.ds(base, 8)

    def split_centroids(it, cols):
        c = cur[it, :, cols]
        hi, lo = split(c)
        cs[0:K, cols] = hi
        cs[K : 2 * K, cols] = lo
        return 0.5 * jnp.sum(c * c, axis=1, keepdims=True)

    def stats(it, n, l, r):
        i = r - CHUNKS[n][0]
        m = jnp.max(l, axis=0, keepdims=True)
        p = jnp.exp(l - m)
        s = jnp.sum(p, axis=0, keepdims=True)
        pbuf[r] = p
        msts[n][i : i + 1] = m
        ests[n][it, i : i + 1] = m + jnp.log(s)

    def product(rows, cols):
        both = dot(cs[:, cols], xv[rows, cols], NT)
        return both[0:K] + both[K : 2 * K]

    def logits(it, n):
        lo, hi = CHUNKS[n]
        for r0 in range(lo, hi, 2):
            size = min(2, hi - r0)
            rows = pl.ds(r0 * PIECE, size * PIECE)
            if it == 0:
                loads[r0 // 2].wait()
            l = product(rows, pl.ds(0, D) if it == 0 else far_cols(1)) - offset
            for j in range(size):
                part = l[:, j * PIECE : (j + 1) * PIECE]
                stats(it, n, part if it == 0 else part + pbuf[r0 + j], r0 + j)

    def z_push(it, n):
        for device in along_z:
            push(ests[n].at[it], zrecvs[n].at[it, z], z_send.at[it, n], z_recv.at[it, n], device)
        zrecvs[n][it, z] = ests[n][it]

    def z_join(it, n):
        await_bytes(zrecvs[n].at[it, pl.ds(0, Z - 1)], z_recv.at[it, n])
        e = zrecvs[n][it]
        m = jnp.max(e, axis=0)
        energies[n][it] = m + jnp.log(jnp.sum(jnp.exp(e - m[None]), axis=0))

    def weigh(it, n):
        lo, hi = CHUNKS[n]
        f = jnp.exp(msts[n][...] - energies[n][it])
        for r in range(lo, hi):
            w = pbuf[r] * f[r - lo : r - lo + 1]
            hi_w, lo_w = split(w)
            cols = pl.ds(r * PIECE, PIECE)
            ws[0:K, cols] = hi_w
            ws[K : 2 * K, cols] = lo_w
            macc[...] += w

    def numer(n, cols):
        lo, hi = CHUNKS[n]
        rows = pl.ds(lo * PIECE, (hi - lo) * PIECE)
        both = dot(ws[:, rows], xv[rows, cols], NN)
        return both[0:K] + both[K : 2 * K]

    load_c.wait()
    offset = split_centroids(0, pl.ds(0, D))
    for it in range(ITERS):
        for n in range(2):
            logits(it, n)
            if it == 0 and n == 0:
                pl.semaphore_wait(barrier, len(peers))
            z_push(it, n)
        macc[...] = jnp.zeros_like(macc)
        z_join(it, 0)
        weigh(it, 0)
        for q in range(Q):
            nacc[:, far_cols(q)] = numer(0, far_cols(q))
        for q in range(Q):
            nacc[:, own_cols(q)] = numer(0, own_cols(q))
        z_join(it, 1)
        weigh(it, 1)

        mass = jnp.sum(macc[...], axis=1, keepdims=True)
        eye = lax.broadcasted_iota(jnp.int32, (K, K), 0) == lax.broadcasted_iota(jnp.int32, (K, K), 1)
        mbuf[it, 0] = jnp.sum(jnp.where(eye, mass, 0.0), axis=0, keepdims=True)
        push(mbuf.at[it, 0], mr0.at[it, 0], m_send.at[it, 0], m_recv.at[it, 0], other)

        for q in range(Q):
            nsend[it, q] = nacc[:, far_cols(q)] + numer(1, far_cols(q))
            push(nsend.at[it, q], crecv.at[it, q], c_send.at[it, q], c_recv.at[it, q], other)

        for q in range(Q):
            part = nacc[:, own_cols(q)] + numer(1, own_cols(q))
            if q == 0:
                await_bytes(mr0.at[it, 0], m_recv.at[it, 0])
                mbuf[it, 1] = mbuf[it, 0] + mr0[it, 0]
                for d, device in enumerate(planes):
                    push(mbuf.at[it, 1], mr1.at[it, d], m_send.at[it, 1], m_recv.at[it, 1], device)
            await_bytes(crecv.at[it, q], c_recv.at[it, q])
            sbuf[it, q] = part + crecv[it, q]
            for d, (c, device) in enumerate(zip(chips, planes)):
                rows = pl.ds(pl.multiple_of(c * 8, 8), 8)
                push(sbuf.at[it, q, rows], arecv.at[it, q, d], a_send.at[it, q], a_recv.at[it, q], device)

        await_bytes(mr1.at[it], m_recv.at[it, 1])
        total = mbuf[it, 1] + jnp.sum(mr1[it], axis=0)
        lane = lax.broadcasted_iota(jnp.int32, (8, K), 1)
        want = lax.broadcasted_iota(jnp.int32, (8, K), 0) + base
        denom = jnp.sum(jnp.where(lane == want, total, 0.0), axis=1, keepdims=True) + PRIOR

        fresh = cur.at[it + 1] if it + 1 < ITERS else out_c
        for q in range(Q):
            await_bytes(arecv.at[it, q], a_recv.at[it, q])
            got = sbuf[it, q, mine] + jnp.sum(arecv[it, q], axis=0)
            cols = own_cols(q)
            fresh[mine, cols] = (got + PRIOR * cur[it, mine, cols]) / denom
            block = fresh.at[mine, cols]
            for device in planes:
                push(block, block, g_send.at[it, q], g_recv.at[it, q], device)
        def partial(parts, add):
            for r0 in range(0, ROWS // PIECE, 2):
                size = min(2, ROWS // PIECE - r0)
                l = sum(product(pl.ds(r0 * PIECE, size * PIECE), cols) for cols in parts)
                for j in range(size):
                    new = l[:, j * PIECE : (j + 1) * PIECE]
                    pbuf[r0 + j] = pbuf[r0 + j] + new if add else new

        more = it + 1 < ITERS
        for q in range(Q):
            await_bytes(fresh.at[pl.ds(0, 120), own_cols(q)], g_recv.at[it, q])
            block = fresh.at[:, own_cols(q)]
            push(block, block, gc_send.at[it, q], gc_recv.at[it, q], other)
            if more and q == 0:
                offset = split_centroids(it + 1, own_cols(0))
                partial([own_cols(0)], False)
        await_bytes(fresh.at[:, far_cols(0)], gc_recv.at[it, 0])
        if more:
            offset = offset + split_centroids(it + 1, own_cols(1)) + split_centroids(it + 1, far_cols(0))
            partial([own_cols(1), far_cols(0)], True)
        await_bytes(fresh.at[:, far_cols(1)], gc_recv.at[it, 1])
        if more:
            offset = offset + split_centroids(it + 1, far_cols(1))

    for n, (lo, hi) in enumerate(CHUNKS):
        out_e[lo:hi] = energies[n][ITERS - 1]

    for it in range(ITERS):
        for n in range(2):
            await_bytes(zrecvs[n].at[it, pl.ds(0, Z - 1)], z_send.at[it, n])
        await_bytes(mr0.at[it, 0], m_send.at[it, 0])
        await_bytes(mr1.at[it], m_send.at[it, 1])
        for q in range(Q):
            await_bytes(crecv.at[it, q], c_send.at[it, q])
            await_bytes(arecv.at[it, q], a_send.at[it, q])
            await_bytes(arecv.at[it, q], g_send.at[it, q])
            await_bytes(crecv.at[it, q], gc_send.at[it, q])


def local(embeddings, centroids):
    f32, bf16 = jnp.float32, jnp.bfloat16
    pieces = ROWS // PIECE
    sizes = [hi - lo for lo, hi in CHUNKS]
    vm = pltpu.VMEM
    dma = pltpu.SemaphoreType.DMA
    new, energy = pl.pallas_call(
        kernel,
        out_shape=(
            jax.ShapeDtypeStruct((K, D), f32),
            jax.ShapeDtypeStruct((pieces, PIECE), f32),
        ),
        in_specs=[pl.BlockSpec(memory_space=pl.ANY)] * 2,
        out_specs=(pl.BlockSpec(memory_space=pltpu.VMEM),) * 2,
        scratch_shapes=[
            [vm((v, PIECE), f32) for v in sizes],
            [vm((ITERS, v, PIECE), f32) for v in sizes],
            [vm((ITERS, v, PIECE), f32) for v in sizes],
            [vm((ITERS, Z, v, PIECE), f32) for v in sizes],
            vm((ROWS, D), bf16),
            vm((ITERS, K, D), f32),
            vm((2 * K, D), bf16),
            vm((pieces, K, PIECE), f32),
            vm((2 * K, ROWS), bf16),
            vm((K, PIECE), f32),
            vm((K, D), f32),
            vm((ITERS, Q, K, CW), f32),
            vm((ITERS, Q, K, CW), f32),
            vm((ITERS, Q, K, CW), f32),
            vm((ITERS, Q, N * N - 1, 8, CW), f32),
            vm((ITERS, 2, 1, K), f32),
            vm((ITERS, 1, 1, K), f32),
            vm((ITERS, N * N - 1, 1, K), f32),
            dma((9,)),
            dma((ITERS, 2)),
            dma((ITERS, 2)),
        ]
        + [dma((ITERS, Q))] * 8
        + [dma((ITERS, 2))] * 2,
        compiler_params=pltpu.CompilerParams(
            collective_id=0, has_side_effects=True, vmem_limit_bytes=53 * 1024 * 1024
        ),
        cost_estimate=pl.CostEstimate(flops=4 * 10**9, bytes_accessed=5 * 10**6, transcendentals=10**6),
    )(embeddings, centroids)
    return new, energy.reshape(ROWS)


def solution(mesh):
    in_specs = (P("dp", None), P("cent", None))
    out_specs = (P("cent", None), P("dp"))
    return jax.shard_map(local, mesh=mesh, in_specs=in_specs, out_specs=out_specs, check_vma=False)
```

```python
import jax
import jax.numpy as jnp
from jax import lax
from jax.experimental import pallas as pl
from jax.experimental.pallas import tpu as pltpu
from jax.sharding import PartitionSpec as P

MESH = pl.DeviceIdType.MESH
ITERS = 2
PRIOR = 2.0
N = 4
Z = 16
ROWS = 1920
D = 1024
K = 128
PIECE = 128
HALF = D // 2
Q = 2
CW = HALF // Q
CHUNKS = ((0, 8), (8, 15))
NT = (((1,), (1,)), ((), ()))
NN = (((1,), (0,)), ((), ()))


def dot(a, b, dims):
    return lax.dot_general(a, b, dims, preferred_element_type=jnp.float32)


def split(v):
    hi = v.astype(jnp.bfloat16)
    lo = (v - hi.astype(jnp.float32)).astype(jnp.bfloat16)
    return hi, lo


def kernel(
    x_hbm, c_hbm, out_c, out_e,
    msts, ests, energies, zrecvs,
    xv, cur, cs, pbuf, ws, macc,
    nacc, nsend, crecv, sbuf, arecv, mbuf, mr0, mr1,
    ld, z_send, z_recv,
    c_send, c_recv, a_send, a_recv, g_send, g_recv, gc_send, gc_recv,
    m_send, m_recv,
):
    dp = lax.axis_index("dp")
    z = lax.axis_index("cent")
    core = lax.rem(dp, 2)
    chip = dp // 2
    cx = lax.rem(chip, N)
    cy = chip // N
    other = (dp + 1 - 2 * core, z)

    def chip_at(dx, dy):
        return lax.rem(cy + dy, N) * N + lax.rem(cx + dx, N)

    moves = [(dx, dy) for dx in range(N) for dy in range(N) if dx or dy]
    moves.sort(key=lambda v: -(min(v[0], N - v[0]) + min(v[1], N - v[1])))
    chips = [chip_at(dx + core * (2 * N - 2 * dx), dy + core * (2 * N - 2 * dy)) for dx, dy in moves]
    planes = [(2 * c + core, z) for c in chips]
    along_z = [(dp, lax.rem(z + d + core * (2 * Z - 2 * d), Z)) for d in sorted(range(1, Z), key=lambda d: -min(d, Z - d))]

    def push(src, dst, send, recv, device):
        pltpu.make_async_remote_copy(
            src_ref=src, dst_ref=dst, send_sem=send, recv_sem=recv,
            device_id=device, device_id_type=MESH,
        ).start()

    def await_bytes(ref, sem):
        pltpu.make_async_copy(ref, ref, sem).wait()

    load_c = pltpu.make_async_copy(c_hbm, cur.at[0], ld.at[0])
    load_c.start()
    loads = []
    for r0 in range(0, ROWS // PIECE, 2):
        rows = pl.ds(r0 * PIECE, min(2, ROWS // PIECE - r0) * PIECE)
        loads.append(pltpu.make_async_copy(x_hbm.at[rows], xv.at[rows], ld.at[1 + r0 // 2]))
        loads[-1].start()

    barrier = pltpu.get_barrier_semaphore()
    peers = [other] + planes + along_z
    for device in peers:
        pl.semaphore_signal(barrier, inc=1, device_id=device, device_id_type=MESH)

    def own_cols(q):
        return pl.ds(pl.multiple_of(core * HALF + q * CW, CW), CW)

    def far_cols(q):
        return pl.ds(pl.multiple_of((1 - core) * HALF + q * CW, CW), CW)

    base = pl.multiple_of(chip * 8, 8)
    mine = pl.ds(base, 8)

    def split_centroids(it, cols):
        c = cur[it, :, cols]
        hi, lo = split(c)
        cs[0:K, cols] = hi
        cs[K : 2 * K, cols] = lo
        return 0.5 * jnp.sum(c * c, axis=1, keepdims=True)

    def stats(it, n, l, r):
        i = r - CHUNKS[n][0]
        m = jnp.max(l, axis=0, keepdims=True)
        p = jnp.exp(l - m)
        s = jnp.sum(p, axis=0, keepdims=True)
        pbuf[r] = p
        msts[n][i : i + 1] = m
        ests[n][it, i : i + 1] = m + jnp.log(s)

    def product(rows, cols):
        both = dot(cs[:, cols], xv[rows, cols], NT)
        return both[0:K] + both[K : 2 * K]

    def logits(it, n):
        lo, hi = CHUNKS[n]
        for r0 in range(lo, hi, 2):
            size = min(2, hi - r0)
            rows = pl.ds(r0 * PIECE, size * PIECE)
            if it == 0:
                loads[r0 // 2].wait()
            l = product(rows, pl.ds(0, D) if it == 0 else far_cols(1)) - offset
            for j in range(size):
                part = l[:, j * PIECE : (j + 1) * PIECE]
                stats(it, n, part if it == 0 else part + pbuf[r0 + j], r0 + j)

    def z_push(it, n):
        for device in along_z:
            push(ests[n].at[it], zrecvs[n].at[it, z], z_send.at[it, n], z_recv.at[it, n], device)
        zrecvs[n][it, z] = ests[n][it]

    def z_join(it, n):
        await_bytes(zrecvs[n].at[it, pl.ds(0, Z - 1)], z_recv.at[it, n])
        e = zrecvs[n][it]
        m = jnp.max(e, axis=0)
        energies[n][it] = m + jnp.log(jnp.sum(jnp.exp(e - m[None]), axis=0))

    def weigh(it, n):
        lo, hi = CHUNKS[n]
        f = jnp.exp(msts[n][...] - energies[n][it])
        for r in range(lo, hi):
            w = pbuf[r] * f[r - lo : r - lo + 1]
            hi_w, lo_w = split(w)
            cols = pl.ds(r * PIECE, PIECE)
            ws[0:K, cols] = hi_w
            ws[K : 2 * K, cols] = lo_w
            macc[...] += w

    def numer(n, cols):
        lo, hi = CHUNKS[n]
        rows = pl.ds(lo * PIECE, (hi - lo) * PIECE)
        both = dot(ws[:, rows], xv[rows, cols], NN)
        return both[0:K] + both[K : 2 * K]

    load_c.wait()
    offset = split_centroids(0, pl.ds(0, D))
    for it in range(ITERS):
        for n in range(2):
            logits(it, n)
            if it == 0 and n == 0:
                pl.semaphore_wait(barrier, len(peers))
            z_push(it, n)
        macc[...] = jnp.zeros_like(macc)
        z_join(it, 0)
        weigh(it, 0)
        for q in range(Q):
            nacc[:, far_cols(q)] = numer(0, far_cols(q))
        for q in range(Q):
            nacc[:, own_cols(q)] = numer(0, own_cols(q))
        z_join(it, 1)
        weigh(it, 1)

        mass = jnp.sum(macc[...], axis=1, keepdims=True)
        eye = lax.broadcasted_iota(jnp.int32, (K, K), 0) == lax.broadcasted_iota(jnp.int32, (K, K), 1)
        mbuf[it, 0] = jnp.sum(jnp.where(eye, mass, 0.0), axis=0, keepdims=True)
        push(mbuf.at[it, 0], mr0.at[it, 0], m_send.at[it, 0], m_recv.at[it, 0], other)

        for q in range(Q):
            nsend[it, q] = nacc[:, far_cols(q)] + numer(1, far_cols(q))
            push(nsend.at[it, q], crecv.at[it, q], c_send.at[it, q], c_recv.at[it, q], other)

        for q in range(Q):
            part = nacc[:, own_cols(q)] + numer(1, own_cols(q))
            if q == 0:
                await_bytes(mr0.at[it, 0], m_recv.at[it, 0])
                mbuf[it, 1] = mbuf[it, 0] + mr0[it, 0]
                for d, device in enumerate(planes):
                    push(mbuf.at[it, 1], mr1.at[it, d], m_send.at[it, 1], m_recv.at[it, 1], device)
            await_bytes(crecv.at[it, q], c_recv.at[it, q])
            sbuf[it, q] = part + crecv[it, q]
            for d, (c, device) in enumerate(zip(chips, planes)):
                rows = pl.ds(pl.multiple_of(c * 8, 8), 8)
                push(sbuf.at[it, q, rows], arecv.at[it, q, d], a_send.at[it, q], a_recv.at[it, q], device)

        await_bytes(mr1.at[it], m_recv.at[it, 1])
        total = mbuf[it, 1] + jnp.sum(mr1[it], axis=0)
        lane = lax.broadcasted_iota(jnp.int32, (8, K), 1)
        want = lax.broadcasted_iota(jnp.int32, (8, K), 0) + base
        denom = jnp.sum(jnp.where(lane == want, total, 0.0), axis=1, keepdims=True) + PRIOR

        fresh = cur.at[it + 1] if it + 1 < ITERS else out_c
        for q in range(Q):
            await_bytes(arecv.at[it, q], a_recv.at[it, q])
            got = sbuf[it, q, mine] + jnp.sum(arecv[it, q], axis=0)
            cols = own_cols(q)
            fresh[mine, cols] = (got + PRIOR * cur[it, mine, cols]) / denom
            block = fresh.at[mine, cols]
            for device in planes:
                push(block, block, g_send.at[it, q], g_recv.at[it, q], device)
        def partial(parts, add):
            for r0 in range(0, ROWS // PIECE, 2):
                size = min(2, ROWS // PIECE - r0)
                l = sum(product(pl.ds(r0 * PIECE, size * PIECE), cols) for cols in parts)
                for j in range(size):
                    new = l[:, j * PIECE : (j + 1) * PIECE]
                    pbuf[r0 + j] = pbuf[r0 + j] + new if add else new

        more = it + 1 < ITERS
        for q in range(Q):
            await_bytes(fresh.at[pl.ds(0, 120), own_cols(q)], g_recv.at[it, q])
            block = fresh.at[:, own_cols(q)]
            push(block, block, gc_send.at[it, q], gc_recv.at[it, q], other)
            if more and q == 0:
                offset = split_centroids(it + 1, own_cols(0))
                partial([own_cols(0)], False)
        await_bytes(fresh.at[:, far_cols(0)], gc_recv.at[it, 0])
        if more:
            offset = offset + split_centroids(it + 1, own_cols(1)) + split_centroids(it + 1, far_cols(0))
            partial([own_cols(1), far_cols(0)], True)
        await_bytes(fresh.at[:, far_cols(1)], gc_recv.at[it, 1])
        if more:
            offset = offset + split_centroids(it + 1, far_cols(1))

    for n, (lo, hi) in enumerate(CHUNKS):
        out_e[lo:hi] = energies[n][ITERS - 1]

    for it in range(ITERS):
        for n in range(2):
            await_bytes(zrecvs[n].at[it, pl.ds(0, Z - 1)], z_send.at[it, n])
        await_bytes(mr0.at[it, 0], m_send.at[it, 0])
        await_bytes(mr1.at[it], m_send.at[it, 1])
        for q in range(Q):
            await_bytes(crecv.at[it, q], c_send.at[it, q])
            await_bytes(arecv.at[it, q], a_send.at[it, q])
            await_bytes(arecv.at[it, q], g_send.at[it, q])
            await_bytes(crecv.at[it, q], gc_send.at[it, q])


def local(embeddings, centroids):
    f32, bf16 = jnp.float32, jnp.bfloat16
    pieces = ROWS // PIECE
    sizes = [hi - lo for lo, hi in CHUNKS]
    vm = pltpu.VMEM
    dma = pltpu.SemaphoreType.DMA
    new, energy = pl.pallas_call(
        kernel,
        out_shape=(
            jax.ShapeDtypeStruct((K, D), f32),
            jax.ShapeDtypeStruct((pieces, PIECE), f32),
        ),
        in_specs=[pl.BlockSpec(memory_space=pl.ANY)] * 2,
        out_specs=(pl.BlockSpec(memory_space=pltpu.VMEM),) * 2,
        scratch_shapes=[
            [vm((v, PIECE), f32) for v in sizes],
            [vm((ITERS, v, PIECE), f32) for v in sizes],
            [vm((ITERS, v, PIECE), f32) for v in sizes],
            [vm((ITERS, Z, v, PIECE), f32) for v in sizes],
            vm((ROWS, D), bf16),
            vm((ITERS, K, D), f32),
            vm((2 * K, D), bf16),
            vm((pieces, K, PIECE), f32),
            vm((2 * K, ROWS), bf16),
            vm((K, PIECE), f32),
            vm((K, D), f32),
            vm((ITERS, Q, K, CW), f32),
            vm((ITERS, Q, K, CW), f32),
            vm((ITERS, Q, K, CW), f32),
            vm((ITERS, Q, N * N - 1, 8, CW), f32),
            vm((ITERS, 2, 1, K), f32),
            vm((ITERS, 1, 1, K), f32),
            vm((ITERS, N * N - 1, 1, K), f32),
            dma((9,)),
            dma((ITERS, 2)),
            dma((ITERS, 2)),
        ]
        + [dma((ITERS, Q))] * 8
        + [dma((ITERS, 2))] * 2,
        compiler_params=pltpu.CompilerParams(
            collective_id=0, has_side_effects=True, vmem_limit_bytes=53 * 1024 * 1024
        ),
        cost_estimate=pl.CostEstimate(flops=4 * 10**9, bytes_accessed=5 * 10**6, transcendentals=10**6),
    )(embeddings, centroids)
    return new, energy.reshape(ROWS)


def solution(mesh):
    in_specs = (P("dp", None), P("cent", None))
    out_specs = (P("cent", None), P("dp"))
    return jax.shard_map(local, mesh=mesh, in_specs=in_specs, out_specs=out_specs, check_vma=False)
```

```python
import jax
import jax.numpy as jnp
from jax import lax
from jax.experimental import pallas as pl
from jax.experimental.pallas import tpu as pltpu
from jax.sharding import PartitionSpec as P

MESH = pl.DeviceIdType.MESH
ITERS = 2
PRIOR = 2.0
N = 4
Z = 16
ROWS = 1920
D = 1024
K = 128
PIECE = 128
HALF = D // 2
Q = 2
CW = HALF // Q
CHUNKS = ((0, 10), (10, 15))
NT = (((1,), (1,)), ((), ()))
NN = (((1,), (0,)), ((), ()))


def dot(a, b, dims):
    return lax.dot_general(a, b, dims, preferred_element_type=jnp.float32)


def split(v):
    hi = v.astype(jnp.bfloat16)
    lo = (v - hi.astype(jnp.float32)).astype(jnp.bfloat16)
    return hi, lo


def kernel(
    x_hbm, c_hbm, out_c, out_e,
    msts, ests, energies, zrecvs,
    xv, cur, cs, pbuf, ws, macc,
    nacc, nsend, crecv, sbuf, arecv, mbuf, mr0, mr1,
    ld, z_send, z_recv,
    c_send, c_recv, a_send, a_recv, g_send, g_recv, gc_send, gc_recv,
    m_send, m_recv,
):
    dp = lax.axis_index("dp")
    z = lax.axis_index("cent")
    core = lax.rem(dp, 2)
    chip = dp // 2
    cx = lax.rem(chip, N)
    cy = chip // N
    other = (dp + 1 - 2 * core, z)

    def chip_at(dx, dy):
        return lax.rem(cy + dy, N) * N + lax.rem(cx + dx, N)

    moves = [(dx, dy) for dx in range(N) for dy in range(N) if dx or dy]
    moves.sort(key=lambda v: -(min(v[0], N - v[0]) + min(v[1], N - v[1])))
    chips = [chip_at(dx, dy) for dx, dy in moves]
    planes = [(2 * c + core, z) for c in chips]
    along_z = [(dp, lax.rem(z + d, Z)) for d in sorted(range(1, Z), key=lambda d: -min(d, Z - d))]

    def push(src, dst, send, recv, device):
        pltpu.make_async_remote_copy(
            src_ref=src, dst_ref=dst, send_sem=send, recv_sem=recv,
            device_id=device, device_id_type=MESH,
        ).start()

    def await_bytes(ref, sem):
        pltpu.make_async_copy(ref, ref, sem).wait()

    load_c = pltpu.make_async_copy(c_hbm, cur.at[0], ld.at[0])
    load_c.start()
    loads = []
    for r0 in range(0, ROWS // PIECE, 2):
        rows = pl.ds(r0 * PIECE, min(2, ROWS // PIECE - r0) * PIECE)
        loads.append(pltpu.make_async_copy(x_hbm.at[rows], xv.at[rows], ld.at[1 + r0 // 2]))
        loads[-1].start()

    barrier = pltpu.get_barrier_semaphore()
    peers = [other] + planes + along_z
    for device in peers:
        pl.semaphore_signal(barrier, inc=1, device_id=device, device_id_type=MESH)

    def own_cols(q):
        return pl.ds(pl.multiple_of(core * HALF + q * CW, CW), CW)

    def far_cols(q):
        return pl.ds(pl.multiple_of((1 - core) * HALF + q * CW, CW), CW)

    base = pl.multiple_of(chip * 8, 8)
    mine = pl.ds(base, 8)

    def split_centroids(it, cols):
        c = cur[it, :, cols]
        hi, lo = split(c)
        cs[0:K, cols] = hi
        cs[K : 2 * K, cols] = lo
        return 0.5 * jnp.sum(c * c, axis=1, keepdims=True)

    def stats(it, n, l, r):
        i = r - CHUNKS[n][0]
        m = jnp.max(l, axis=0, keepdims=True)
        p = jnp.exp(l - m)
        s = jnp.sum(p, axis=0, keepdims=True)
        pbuf[r] = p
        msts[n][i : i + 1] = m
        ests[n][it, i : i + 1] = m + jnp.log(s)

    def product(rows, cols):
        both = dot(cs[:, cols], xv[rows, cols], NT)
        return both[0:K] + both[K : 2 * K]

    def logits(it, n):
        lo, hi = CHUNKS[n]
        for r0 in range(lo, hi, 2):
            size = min(2, hi - r0)
            rows = pl.ds(r0 * PIECE, size * PIECE)
            if it == 0:
                loads[r0 // 2].wait()
            l = product(rows, pl.ds(0, D) if it == 0 else far_cols(1)) - offset
            for j in range(size):
                part = l[:, j * PIECE : (j + 1) * PIECE]
                stats(it, n, part if it == 0 else part + pbuf[r0 + j], r0 + j)

    def z_push(it, n):
        for device in along_z:
            push(ests[n].at[it], zrecvs[n].at[it, z], z_send.at[it, n], z_recv.at[it, n], device)
        zrecvs[n][it, z] = ests[n][it]

    def z_join(it, n):
        await_bytes(zrecvs[n].at[it, pl.ds(0, Z - 1)], z_recv.at[it, n])
        e = zrecvs[n][it]
        m = jnp.max(e, axis=0)
        energies[n][it] = m + jnp.log(jnp.sum(jnp.exp(e - m[None]), axis=0))

    def weigh(it, n):
        lo, hi = CHUNKS[n]
        f = jnp.exp(msts[n][...] - energies[n][it])
        for r in range(lo, hi):
            w = pbuf[r] * f[r - lo : r - lo + 1]
            hi_w, lo_w = split(w)
            cols = pl.ds(r * PIECE, PIECE)
            ws[0:K, cols] = hi_w
            ws[K : 2 * K, cols] = lo_w
            macc[...] += w

    def numer(n, cols):
        lo, hi = CHUNKS[n]
        rows = pl.ds(lo * PIECE, (hi - lo) * PIECE)
        both = dot(ws[:, rows], xv[rows, cols], NN)
        return both[0:K] + both[K : 2 * K]

    load_c.wait()
    offset = split_centroids(0, pl.ds(0, D))
    for it in range(ITERS):
        for n in range(2):
            logits(it, n)
            if it == 0 and n == 0:
                pl.semaphore_wait(barrier, len(peers))
            z_push(it, n)
        macc[...] = jnp.zeros_like(macc)
        z_join(it, 0)
        weigh(it, 0)
        for q in range(Q):
            nacc[:, far_cols(q)] = numer(0, far_cols(q))
        for q in range(Q):
            nacc[:, own_cols(q)] = numer(0, own_cols(q))
        z_join(it, 1)
        weigh(it, 1)

        mass = jnp.sum(macc[...], axis=1, keepdims=True)
        eye = lax.broadcasted_iota(jnp.int32, (K, K), 0) == lax.broadcasted_iota(jnp.int32, (K, K), 1)
        mbuf[it, 0] = jnp.sum(jnp.where(eye, mass, 0.0), axis=0, keepdims=True)
        push(mbuf.at[it, 0], mr0.at[it, 0], m_send.at[it, 0], m_recv.at[it, 0], other)

        for q in range(Q):
            nsend[it, q] = nacc[:, far_cols(q)] + numer(1, far_cols(q))
            push(nsend.at[it, q], crecv.at[it, q], c_send.at[it, q], c_recv.at[it, q], other)

        for q in range(Q):
            part = nacc[:, own_cols(q)] + numer(1, own_cols(q))
            if q == 0:
                await_bytes(mr0.at[it, 0], m_recv.at[it, 0])
                mbuf[it, 1] = mbuf[it, 0] + mr0[it, 0]
                for d, device in enumerate(planes):
                    push(mbuf.at[it, 1], mr1.at[it, d], m_send.at[it, 1], m_recv.at[it, 1], device)
            await_bytes(crecv.at[it, q], c_recv.at[it, q])
            sbuf[it, q] = part + crecv[it, q]
            for d, (c, device) in enumerate(zip(chips, planes)):
                rows = pl.ds(pl.multiple_of(c * 8, 8), 8)
                push(sbuf.at[it, q, rows], arecv.at[it, q, d], a_send.at[it, q], a_recv.at[it, q], device)

        await_bytes(mr1.at[it], m_recv.at[it, 1])
        total = mbuf[it, 1] + jnp.sum(mr1[it], axis=0)
        lane = lax.broadcasted_iota(jnp.int32, (8, K), 1)
        want = lax.broadcasted_iota(jnp.int32, (8, K), 0) + base
        denom = jnp.sum(jnp.where(lane == want, total, 0.0), axis=1, keepdims=True) + PRIOR

        fresh = cur.at[it + 1] if it + 1 < ITERS else out_c
        for q in range(Q):
            await_bytes(arecv.at[it, q], a_recv.at[it, q])
            got = sbuf[it, q, mine] + jnp.sum(arecv[it, q], axis=0)
            cols = own_cols(q)
            fresh[mine, cols] = (got + PRIOR * cur[it, mine, cols]) / denom
            block = fresh.at[mine, cols]
            for device in planes:
                push(block, block, g_send.at[it, q], g_recv.at[it, q], device)
        def partial(parts, add):
            for r0 in range(0, ROWS // PIECE, 2):
                size = min(2, ROWS // PIECE - r0)
                l = sum(product(pl.ds(r0 * PIECE, size * PIECE), cols) for cols in parts)
                for j in range(size):
                    new = l[:, j * PIECE : (j + 1) * PIECE]
                    pbuf[r0 + j] = pbuf[r0 + j] + new if add else new

        more = it + 1 < ITERS
        for q in range(Q):
            await_bytes(fresh.at[pl.ds(0, 120), own_cols(q)], g_recv.at[it, q])
            block = fresh.at[:, own_cols(q)]
            push(block, block, gc_send.at[it, q], gc_recv.at[it, q], other)
            if more and q == 0:
                offset = split_centroids(it + 1, own_cols(0))
                partial([own_cols(0)], False)
        await_bytes(fresh.at[:, far_cols(0)], gc_recv.at[it, 0])
        if more:
            offset = offset + split_centroids(it + 1, own_cols(1)) + split_centroids(it + 1, far_cols(0))
            partial([own_cols(1), far_cols(0)], True)
        await_bytes(fresh.at[:, far_cols(1)], gc_recv.at[it, 1])
        if more:
            offset = offset + split_centroids(it + 1, far_cols(1))

    for n, (lo, hi) in enumerate(CHUNKS):
        out_e[lo:hi] = energies[n][ITERS - 1]

    for it in range(ITERS):
        for n in range(2):
            await_bytes(zrecvs[n].at[it, pl.ds(0, Z - 1)], z_send.at[it, n])
        await_bytes(mr0.at[it, 0], m_send.at[it, 0])
        await_bytes(mr1.at[it], m_send.at[it, 1])
        for q in range(Q):
            await_bytes(crecv.at[it, q], c_send.at[it, q])
            await_bytes(arecv.at[it, q], a_send.at[it, q])
            await_bytes(arecv.at[it, q], g_send.at[it, q])
            await_bytes(crecv.at[it, q], gc_send.at[it, q])


def local(embeddings, centroids):
    f32, bf16 = jnp.float32, jnp.bfloat16
    pieces = ROWS // PIECE
    sizes = [hi - lo for lo, hi in CHUNKS]
    vm = pltpu.VMEM
    dma = pltpu.SemaphoreType.DMA
    new, energy = pl.pallas_call(
        kernel,
        out_shape=(
            jax.ShapeDtypeStruct((K, D), f32),
            jax.ShapeDtypeStruct((pieces, PIECE), f32),
        ),
        in_specs=[pl.BlockSpec(memory_space=pl.ANY)] * 2,
        out_specs=(pl.BlockSpec(memory_space=pltpu.VMEM),) * 2,
        scratch_shapes=[
            [vm((v, PIECE), f32) for v in sizes],
            [vm((ITERS, v, PIECE), f32) for v in sizes],
            [vm((ITERS, v, PIECE), f32) for v in sizes],
            [vm((ITERS, Z, v, PIECE), f32) for v in sizes],
            vm((ROWS, D), bf16),
            vm((ITERS, K, D), f32),
            vm((2 * K, D), bf16),
            vm((pieces, K, PIECE), f32),
            vm((2 * K, ROWS), bf16),
            vm((K, PIECE), f32),
            vm((K, D), f32),
            vm((ITERS, Q, K, CW), f32),
            vm((ITERS, Q, K, CW), f32),
            vm((ITERS, Q, K, CW), f32),
            vm((ITERS, Q, N * N - 1, 8, CW), f32),
            vm((ITERS, 2, 1, K), f32),
            vm((ITERS, 1, 1, K), f32),
            vm((ITERS, N * N - 1, 1, K), f32),
            dma((9,)),
            dma((ITERS, 2)),
            dma((ITERS, 2)),
        ]
        + [dma((ITERS, Q))] * 8
        + [dma((ITERS, 2))] * 2,
        compiler_params=pltpu.CompilerParams(
            collective_id=0, has_side_effects=True, vmem_limit_bytes=53 * 1024 * 1024
        ),
        cost_estimate=pl.CostEstimate(flops=4 * 10**9, bytes_accessed=5 * 10**6, transcendentals=10**6),
    )(embeddings, centroids)
    return new, energy.reshape(ROWS)


def solution(mesh):
    in_specs = (P("dp", None), P("cent", None))
    out_specs = (P("cent", None), P("dp"))
    return jax.shard_map(local, mesh=mesh, in_specs=in_specs, out_specs=out_specs, check_vma=False)
```
